32 devices in a mesh: wide: 16 (over z, x, core), kv: 2 (over y).
Axes of the slice: x: 2, y: 2, z: 4, core: 2. Of those that a mesh axis runs over, the one named last changes fastest.
Arguments:
- queries: bfloat16 [64, 2, 8192], P('wide', None, 'kv'), may hold values from -14 to 14
- new_kv: bfloat16 [64, 2, 8, 256], P('wide', None, 'kv'), may hold values from -6 to 6
- suffix_cache: bfloat16 [64, 512, 8, 256], P('wide', None, 'kv'), may hold values from -14 to 14
- suffix_len: int32 [64], P('wide'), may hold values from 1 to 512, 24576 in all
- prefix_cache: bfloat16 [8192, 8, 256], P('wide', 'kv'), may hold values from -14 to 14
- prompt_len: int32 [8], replicated, may hold values from 1 to 1024, 4096 in all
- prompt_slot: int32 [8], replicated, may hold values from 0 to 7, each once
- sample_prompt: int32 [64, 1], replicated, may hold values from 0 to 7; in each aligned block of 4 rows (0 to 3, 4 to 7, ...) at most 2 rows name the same one
- out_weight: bfloat16 [8192, 8192], P('kv', 'wide'), may hold values from -0.0625 to 0.0625
Outputs:
- mixed: bfloat16 [64, 2, 8192], P('kv', None, 'wide')
The draws below stay inside these ranges and needn't reach their ends.
Inputs may be any that keep to these rules, and one draw needn't show every extreme that they name: A permutation: prompt p's cache occupies rows prompt_slot[p] * 1024 to prompt_slot[p] * 1024 + 1023 of prefix_cache. `sample_prompt`: sample i is held by wide index i // 4; among the samples of one wide index at most 2 continue the same prompt.
All inputs are finite; a program needn't handle non-finite values. No bound on the sum of `suffix_len` on one device may be relied on, other than what follows from the above.
Results may differ from the reference program's by a relative error of at most 0.0061.
Values may be sent and summed in bfloat16 or wider, within the bound.
A program may use at most 64 MiB of HBM per device.

```python
import math
import jax
import jax.numpy as jnp
import numpy as np
from jax import lax

D = 8192
HQ = 64
KVH = 8
HD = 128
GROUP = 8
STEPS = 2
PSH = 512
SUF = 512
SAMP_DEV = 4
NPROMPT = 8
MOST = 2
PLEN = 1024
NSAMP = 64
N_WIDE = 16


def draw_queries(key, part):
    key = jax.random.fold_in(key, 11)
    key_one = jax.random.fold_in(key, 0)
    full_shape = (NSAMP, STEPS, HQ * HD)
    values = jnp.clip(2.0 * jax.random.normal(key_one, full_shape, jnp.float32), -8.0, 8.0)
    return values.astype(jnp.bfloat16)


def cache_rows(key, blocks, block_len):
    key_one, key_two = jax.random.split(key, 2)
    key_part = jnp.clip(jax.random.normal(key_one, (blocks, block_len, KVH, HD), jnp.float32), -6.0, 6.0)
    value_part = jnp.clip(2.0 * jax.random.normal(key_two, (blocks, block_len, KVH, HD), jnp.float32), -8.0, 8.0)
    return jnp.concatenate([key_part, value_part], axis=-1)


def draw_prefix_cache(key, part):
    key = jax.random.fold_in(key, 23)
    rows = cache_rows(key, NPROMPT * PLEN // PSH, PSH)
    return rows.reshape(NPROMPT * PLEN, KVH, 2 * HD).astype(jnp.bfloat16)


def draw_suffix_cache(key, part):
    key = jax.random.fold_in(key, 37)
    rows = cache_rows(key, NSAMP, SUF)
    return rows.astype(jnp.bfloat16)


def level_of(own_key, extent, shards, low, high):
    loudness = 1.0
    for dim, blocks in shards:
        heights = jax.random.uniform(jax.random.fold_in(jax.random.fold_in(own_key, 6), dim), (blocks,), jnp.float32, low / len(shards), high / len(shards))
        loudness = loudness * jnp.repeat(jnp.exp(heights), extent[dim] // blocks).reshape((-1,) + (1,) * (len(extent) - 1 - dim))
    return loudness


def profile(number_of, total, limit, slope):
    weights = [(1 << 20) // math.isqrt(standing ** slope) + 1 for standing in range(2, number_of + 1)]
    rest, holding = total - limit - (number_of - 1), [1] * (number_of - 1)
    while rest > 0:
        candidates = [i for i in range(number_of - 1) if holding[i] < limit]
        mass, left = sum([weights[i] for i in candidates]), rest
        for i in candidates:
            more = min(limit - holding[i], max(1, left * weights[i] // mass), rest)
            holding[i] = holding[i] + more
            rest = rest - more
    return np.array([limit] + holding)


def uneven(stream_key, amount, total, most, skew):
    if amount == 2:
        one = jax.random.randint(stream_key, (), max(1, total - most), min(most, total - 1) + 1)
        return jnp.stack([one, total - one])
    lengths = jnp.asarray(profile(amount, total, most, skew), jnp.int32)
    couples = (amount - 1) // 2
    donor, receiver = lengths[1:1 + 2 * couples:2], lengths[2:2 + 2 * couples:2]
    room = jnp.minimum(donor - 1, most - receiver)
    shifted = jax.random.randint(jax.random.fold_in(stream_key, 1), (couples,), 0, 1 << 20) % (room + 1)
    lengths = lengths.at[1:1 + 2 * couples:2].set(donor - shifted).at[2:2 + 2 * couples:2].set(receiver + shifted)
    return lengths[jax.random.permutation(jax.random.fold_in(stream_key, 2), amount)]


def deal_out(stream_key, own, number, rows, count, top, reach, skew):
    order = jax.random.permutation(stream_key, count)
    heavy_load, usual = shares(count, rows * top, reach, skew, True), shares(count, rows * top, reach, skew, False)
    places = jnp.arange(count)

    def named(tallies, turn):
        used = int((tallies > 0).sum())
        fixed = max(1, used // 4)
        moved = fixed + (places - fixed + turn * (used - fixed)) % max(1, count - fixed)
        return jnp.zeros((count,), jnp.int32).at[order[jnp.where(places < fixed, places, moved)]].set(jnp.asarray(tallies, jnp.int32))

    tallies = jnp.where(number % 4 == 0, named(heavy_load, number // 4), named(usual, number - number // 4 - 1))
    mixed = jax.random.permutation(jax.random.fold_in(own, 3), count)
    source_of, taker = mixed[0:count // 2 * 2:2], mixed[1:count // 2 * 2:2]
    slack = jnp.minimum(tallies[source_of] - 1, reach - tallies[taker]) // 2
    slack = jnp.where((source_of == order[0]) | (taker == order[0]) | (tallies[taker] == 0), 0, jnp.maximum(slack, 0))
    moved = jax.random.randint(jax.random.fold_in(own, 4), (count // 2,), 0, 1 << 20) % (slack + 1)
    tallies = tallies.at[source_of].add(-moved).at[taker].add(moved)
    items = jnp.searchsorted(jnp.cumsum(tallies), jnp.arange(rows * top), side="right").astype(jnp.int32)
    table = items.reshape(top, rows).T
    table = table[jax.random.permutation(jax.random.fold_in(own, 1), rows)]
    turn = jax.random.randint(jax.random.fold_in(own, 2), (rows, 1), 0, top)
    return jnp.take_along_axis(table, (jnp.arange(top)[None, :] + turn) % top, axis=1)


def shares(amount, total, limit, lean, full):
    loads = [(1 << 20) // math.isqrt(rank ** lean) + 1 for rank in range(1, amount + 1)]
    largest = limit if full else min(limit, max(-(-total // amount), total * loads[0] // sum(loads)))
    least = 1 if total - largest >= amount - 1 else 0
    given, rest = [largest] + [least] * (amount - 1), total - largest - least * (amount - 1)
    while rest > 0:
        candidates = [i for i in range(1, amount) if given[i] < largest] or [i for i in range(1, amount) if given[i] < limit]
        whole, remaining = sum([loads[i] for i in candidates]), rest
        for i in candidates:
            extra = min(limit - given[i], max(1, remaining * loads[i] // whole), rest)
            given[i] = given[i] + extra
            rest = rest - extra
    return np.array(given)


def bell_draw(own_key, dims, spread, most, cuts=(), kind=jnp.bfloat16):
    values = spread * jax.random.normal(own_key, dims, jnp.float32)
    if cuts:
        values = values * level_of(own_key, dims, cuts, -0.22, 0.18)
    return jnp.clip(values, -most, most).astype(kind)


def setup_inputs(seed: int = 0) -> dict:
    key_list = jax.random.split(jax.random.key(seed), 10)
    queries = draw_queries(jax.random.fold_in(key_list[9], 71), 0)
    new_kv = bell_draw(key_list[1], (NSAMP, STEPS, KVH, 2 * HD), 1.5, 6.0, ((0, 16), (2, 2)))
    suffix_cache = draw_suffix_cache(jax.random.fold_in(key_list[9], 71), 0)
    suffix_len = uneven(key_list[3], NSAMP, NSAMP * SUF * 3 // 4, SUF, 1).astype(jnp.int32)
    prefix_cache = draw_prefix_cache(jax.random.fold_in(key_list[9], 71), 0)
    prompt_len = uneven(key_list[5], NPROMPT, NPROMPT * PLEN // 2, PLEN, 2).astype(jnp.int32)
    prompt_slot = jax.random.permutation(key_list[6], NPROMPT).astype(jnp.int32)
    sample_prompt_keys = jax.random.split(jax.random.fold_in(key_list[7], 1), NSAMP // SAMP_DEV)
    sample_prompt_turns = jax.random.permutation(jax.random.fold_in(key_list[7], 3), NSAMP // SAMP_DEV)
    sample_prompt = jax.vmap(lambda own, number: deal_out(jax.random.fold_in(key_list[7], 2), own, number, SAMP_DEV, NPROMPT, 1, MOST, 2))(sample_prompt_keys, sample_prompt_turns).reshape((NSAMP, 1))
    out_weight = bell_draw(key_list[8], (HQ * HD, D), (HQ * HD) ** -0.5, 0.0625, ((0, 2), (1, 16)))
    return {"queries": queries, "new_kv": new_kv, "suffix_cache": suffix_cache, "suffix_len": suffix_len, "prefix_cache": prefix_cache, "prompt_len": prompt_len, "prompt_slot": prompt_slot, "sample_prompt": sample_prompt, "out_weight": out_weight}


def reference(queries, new_kv, suffix_cache, suffix_len, prefix_cache, prompt_len, prompt_slot, sample_prompt, out_weight):
    split_count = N_WIDE // NPROMPT
    scale = HD ** -0.5

    def one_sample(sample_index):
        prompt = sample_prompt[sample_index, 0]
        first_row = (prompt_slot[prompt] * PLEN).astype(jnp.int32)
        prompt_cache = lax.dynamic_slice_in_dim(prefix_cache, first_row, PLEN, 0).astype(jnp.float32)
        query_rows = queries[sample_index].astype(jnp.float32).reshape(STEPS, KVH, GROUP, HD)
        scores = jnp.einsum("tgxd,jgd->tgxj", query_rows, prompt_cache[:, :, :HD]) * scale
        scores = scores.reshape(STEPS, KVH, GROUP, split_count, PSH)
        usable = (jnp.arange(PLEN) < prompt_len[prompt]).reshape(split_count, PSH)
        masked = jnp.where(usable, scores, -1e30)
        seg_max = jnp.max(masked, axis=-1)
        weights = jnp.where(usable, jnp.exp(masked - seg_max[..., None]), 0.0)
        seg_sum = jnp.sum(weights, axis=-1)
        seg_probs = lax.optimization_barrier((weights / jnp.maximum(seg_sum, 1.0)[..., None]).astype(jnp.bfloat16))
        prompt_values = prompt_cache[:, :, HD:].reshape(split_count, PSH, KVH, HD)
        seg_out = jnp.einsum("tgxsj,sjgd->tgxsd", seg_probs.astype(jnp.float32), prompt_values)
        seg_out = lax.optimization_barrier(seg_out.astype(jnp.bfloat16)).astype(jnp.float32)

        local_rows = jnp.concatenate([suffix_cache[sample_index], new_kv[sample_index]], axis=0).astype(jnp.float32)
        local_scores = jnp.einsum("tgxd,jgd->tgxj", query_rows, local_rows[:, :, :HD]) * scale
        positions = jnp.arange(SUF + STEPS)
        step_ids = jnp.arange(STEPS)
        local_ok = jnp.where(positions[None, :] < SUF, positions[None, :] < suffix_len[sample_index], positions[None, :] - SUF <= step_ids[:, None])
        local_ok = local_ok[:, None, None, :]
        local_masked = jnp.where(local_ok, local_scores, -1e30)
        local_max = jnp.max(local_masked, axis=-1)
        local_weights = jnp.where(local_ok, jnp.exp(local_masked - local_max[..., None]), 0.0)
        local_sum = jnp.sum(local_weights, axis=-1)
        local_probs = lax.optimization_barrier((local_weights / local_sum[..., None]).astype(jnp.bfloat16))
        local_out = jnp.einsum("tgxj,jgd->tgxd", local_probs.astype(jnp.float32), local_rows[:, :, HD:])

        overall = jnp.maximum(jnp.max(seg_max, axis=-1), local_max)
        seg_weight = seg_sum * jnp.exp(seg_max - overall[..., None])
        local_weight = local_sum * jnp.exp(local_max - overall)
        numerator = jnp.sum(seg_weight[..., None] * seg_out, axis=3) + local_weight[..., None] * local_out
        denominator = jnp.sum(seg_weight, axis=-1) + local_weight
        attn = (numerator / denominator[..., None]).astype(jnp.bfloat16)
        return attn.reshape(STEPS, HQ * HD)

    attn_all = lax.map(one_sample, jnp.arange(NSAMP))
    mixed = jnp.dot(attn_all.reshape(NSAMP * STEPS, HQ * HD), out_weight, preferred_element_type=jnp.float32)
    return mixed.astype(jnp.bfloat16).reshape(NSAMP, STEPS, D)
```

```python
import functools
import math

import jax
import jax.numpy as jnp
from jax import lax
from jax.experimental import pallas as pl
from jax.experimental.pallas import tpu as pltpu
from jax.sharding import PartitionSpec as P

HD = 128
GROUP = 8
STEPS = 2
PSH = 512
SUF = 512
NPROMPT = 8
MOST = 2


def sample_ranks(prompt_block):
    length = prompt_block.shape[-1]
    earlier = jnp.arange(length)[None, :] < jnp.arange(length)[:, None]
    matching = prompt_block[..., :, None] == prompt_block[..., None, :]
    return jnp.sum(matching & earlier, axis=-1)


def prefix_part(slots, prefix_cache, prompt_rows, segment):
    sources = slots.shape[0]
    item_count = slots.shape[1]
    kv_local = prefix_cache.shape[1]
    batch_rows = sources * item_count * STEPS
    scale = HD ** (-0.5)
    key_rows = prefix_cache[:, :, :HD]
    value_rows = prefix_cache[:, :, HD:]
    usable = segment * PSH + jnp.arange(PSH) < prompt_rows
    block_rows = math.gcd(batch_rows, max(1, 512 // (kv_local * GROUP)))

    def one_block(query_block):
        scores = (
            jnp.einsum("bgxd,jgd->bgxj", query_block, key_rows, preferred_element_type=jnp.float32)
            * scale
        )
        masked = jnp.where(usable, scores, -1e30)
        row_max = jnp.max(masked, axis=-1)
        weights = jnp.where(usable, jnp.exp(masked - row_max[..., None]), 0.0)
        row_sum = jnp.sum(weights, axis=-1)
        weights_bf = (weights / jnp.maximum(row_sum, 1.0)[..., None]).astype(jnp.bfloat16)
        result = jnp.einsum(
            "bgxj,jgd->bgxd", weights_bf, value_rows, preferred_element_type=jnp.float32
        )
        return (result.astype(jnp.bfloat16), row_max, row_sum)

    query_blocks = slots.reshape(batch_rows // block_rows, block_rows, kv_local, GROUP, HD)
    results = lax.map(one_block, query_blocks)
    part_out = results[0].reshape(sources, item_count, -1)
    part_max = results[1].reshape(sources, item_count, -1)
    part_sum = results[2].reshape(sources, item_count, -1)
    part_out = lax.all_to_all(part_out, "wide", split_axis=0, concat_axis=0, tiled=True)
    part_max, part_sum = (
        lax.all_to_all(part_max, "wide", split_axis=0, concat_axis=0, tiled=True),
        lax.all_to_all(part_sum, "wide", split_axis=0, concat_axis=0, tiled=True),
    )
    return (part_out, part_max, part_sum)


def general_device(
    queries,
    new_kv,
    suffix_cache,
    suffix_len,
    prefix_cache,
    prompt_len,
    prompt_slot,
    sample_prompt,
    out_weight,
):
    wide_count = lax.axis_size("wide")
    split_count = wide_count // NPROMPT
    position = lax.axis_index("wide")
    held_rows = queries.shape[0]
    kv_local = new_kv.shape[2]
    scale = HD ** (-0.5)
    prompt_ids = sample_prompt[:, 0]
    my_prompts = lax.dynamic_slice_in_dim(prompt_ids, position * held_rows, held_rows)
    prompt_range = jnp.arange(NPROMPT)
    slot_range = jnp.arange(MOST)
    my_group = jnp.sum(
        jnp.where(my_prompts[:, None] == prompt_range[None, :], prompt_slot[None, :], 0), axis=1
    )
    my_rank = sample_ranks(my_prompts)
    picked = (my_group[:, None, None] == prompt_range[None, :, None]) & (
        my_rank[:, None, None] == slot_range[None, None, :]
    )
    own_group = position // split_count
    segment = position % split_count
    owner_match = prompt_slot == own_group
    prompt_rows = jnp.sum(jnp.where(owner_match, prompt_len, 0))
    own_prompt = jnp.sum(jnp.where(owner_match, prompt_range, 0))
    flat_queries = queries.reshape(held_rows, -1)
    everyone = lax.all_gather(flat_queries, "wide", axis=0, tiled=True)
    blocks = prompt_ids.reshape(wide_count, held_rows)
    block_rank = sample_ranks(blocks)
    chosen = (blocks[:, :, None] == own_prompt) & (
        block_rank[:, :, None] == slot_range[None, None, :]
    )
    incoming = jnp.einsum(
        "hrc,hrx->hcx",
        chosen.astype(jnp.bfloat16),
        everyone.reshape(wide_count, held_rows, -1),
        preferred_element_type=jnp.float32,
    ).astype(jnp.bfloat16)
    part_out, part_max, part_sum = prefix_part(incoming, prefix_cache, prompt_rows, segment)
    picked_bf = picked.astype(jnp.bfloat16)
    picked_f32 = picked.astype(jnp.float32)
    prefix_out = jnp.einsum(
        "rgc,gscx->rsx",
        picked_bf,
        part_out.reshape(NPROMPT, split_count, MOST, -1),
        preferred_element_type=jnp.float32,
    )
    prefix_max = jnp.einsum(
        "rgc,gscy->rsy",
        picked_f32,
        part_max.reshape(NPROMPT, split_count, MOST, -1),
        precision=lax.Precision.HIGHEST,
    )
    prefix_sum = jnp.einsum(
        "rgc,gscy->rsy",
        picked_f32,
        part_sum.reshape(NPROMPT, split_count, MOST, -1),
        precision=lax.Precision.HIGHEST,
    )
    prefix_out = prefix_out.reshape(held_rows, split_count, STEPS, kv_local, GROUP, HD)
    prefix_max = prefix_max.reshape(held_rows, split_count, STEPS, kv_local, GROUP)
    prefix_sum = prefix_sum.reshape(held_rows, split_count, STEPS, kv_local, GROUP)
    query_rows = queries.reshape(held_rows, STEPS, kv_local, GROUP, HD)
    local_rows = jnp.concatenate([suffix_cache, new_kv], axis=1)
    local_scores = (
        jnp.einsum(
            "stgxd,sjgd->stgxj",
            query_rows,
            local_rows[..., :HD],
            preferred_element_type=jnp.float32,
        )
        * scale
    )
    positions = jnp.arange(SUF + STEPS)
    step_ids = jnp.arange(STEPS)
    local_ok = jnp.where(
        positions[None, None, :] < SUF,
        positions[None, None, :] < suffix_len[:, None, None],
        positions[None, None, :] - SUF <= step_ids[None, :, None],
    )
    local_ok = local_ok[:, :, None, None, :]
    local_masked = jnp.where(local_ok, local_scores, -1e30)
    local_max = jnp.max(local_masked, axis=-1)
    local_weights = jnp.where(local_ok, jnp.exp(local_masked - local_max[..., None]), 0.0)
    local_sum = jnp.sum(local_weights, axis=-1)
    local_bf = (local_weights / local_sum[..., None]).astype(jnp.bfloat16)
    local_out = jnp.einsum(
        "stgxj,sjgd->stgxd", local_bf, local_rows[..., HD:], preferred_element_type=jnp.float32
    )
    overall = jnp.maximum(jnp.max(prefix_max, axis=1), local_max)
    seg_weight = prefix_sum * jnp.exp(prefix_max - overall[:, None])
    local_weight = local_sum * jnp.exp(local_max - overall)
    numerator = (
        jnp.sum(seg_weight[..., None] * prefix_out, axis=1) + local_weight[..., None] * local_out
    )
    denominator = jnp.sum(seg_weight, axis=1) + local_weight
    attn = (numerator / denominator[..., None]).astype(jnp.bfloat16).reshape(held_rows, STEPS, -1)
    terms = jnp.einsum(
        "stk,kd->std",
        lax.all_gather(attn, "wide", axis=0, tiled=True),
        out_weight,
        preferred_element_type=jnp.float32,
    )
    summed = lax.psum_scatter(terms, "kv", scatter_dimension=0, tiled=True)
    return summed.astype(jnp.bfloat16)


MESH = pl.DeviceIdType.MESH
CHIPS = 8
HELD = 4
KVL = 4
ROWS = STEPS * GROUP
SPAN = KVL * ROWS
LOCAL = SUF + 128
SCALE = HD ** (-0.5)
NT = (((1,), (1,)), ((), ()))


def fused_kernel(
    slen_ref,
    plen_ref,
    pslot_ref,
    sprompt_ref,
    q_ref,
    new_ref,
    suf_hbm,
    pre_hbm,
    w_hbm,
    o_ref,
    suf,
    pre,
    w,
    split_p,
    turn_p,
    lkv,
    pkv,
    qslot,
    qrecv,
    lo,
    lm,
    ll,
    half_o,
    half_m,
    half_l,
    so_send,
    st_send,
    so_recv,
    st_recv,
    co_send,
    cs_send,
    co_recv,
    cs_recv,
    ag,
    lhs,
    terms,
    y_send,
    y_recv,
    loc_sem,
    q_ss,
    q_rs,
    qf_ss,
    qf_rs,
    x_ss,
    x_rs,
    c_ss,
    c_rs,
    s_ss,
    s_rs,
    z_ss,
    z_rs,
    ax_ss,
    ax_rs,
    ac_ss,
    ac_rs,
    y_ss,
    y_rs,
):
    f32, bf16 = jnp.float32, jnp.bfloat16
    wide = lax.axis_index("wide")
    y = lax.axis_index("kv")
    chip = wide // 2
    core = wide % 2
    zc = chip // 2
    xc = chip % 2
    sibling = (chip * 2 + 1 - core, y)

    def at_chip(c):
        return (c * 2 + core, y)

    local_copies = [pltpu.make_async_copy(pre_hbm, pre, loc_sem.at[0])]
    local_copies += [
        pltpu.make_async_copy(suf_hbm.at[s], suf.at[s], loc_sem.at[1 + s]) for s in range(HELD)
    ]
    local_copies.append(pltpu.make_async_copy(w_hbm, w, loc_sem.at[1 + HELD]))
    for copy in local_copies:
        copy.start()

    barrier = pltpu.get_barrier_semaphore()
    for d in range(1, CHIPS):
        pl.semaphore_signal(
            barrier, inc=1, device_id=at_chip((chip + d) % CHIPS), device_id_type=MESH
        )
    pl.semaphore_signal(barrier, inc=1, device_id=sibling, device_id_type=MESH)
    pl.semaphore_signal(barrier, inc=1, device_id=(wide, 1 - y), device_id_type=MESH)

    prompts = [sprompt_ref[wide * HELD + s] for s in range(HELD)]
    groups = [pslot_ref[p] for p in prompts]
    ranks = []
    for s in range(HELD):
        rank = jnp.int32(0)
        for e in range(s):
            rank = rank + jnp.where(prompts[e] == prompts[s], 1, 0)
        ranks.append(rank)
    for c in range(CHIPS):
        for m in range(MOST):
            pick = jnp.int32(0)
            for s in range(1, HELD):
                pick = pick + jnp.where((groups[s] == c) & (ranks[s] == m), s, 0)
            qslot[c, m * SPAN : (m + 1) * SPAN, :] = q_ref[pick]
    prompt_rows = jnp.int32(0)
    for p in range(NPROMPT):
        prompt_rows = prompt_rows + jnp.where(pslot_ref[p] == chip, plen_ref[p], 0)

    out_row = lax.broadcasted_iota(jnp.int32, (256, 256), 0)
    in_row = lax.broadcasted_iota(jnp.int32, (256, 256), 1)
    split_p[...] = jnp.where(in_row == (out_row & 31) * 8 + (out_row >> 5), 1.0, 0.0).astype(bf16)
    source = (
        ((out_row >> 1) & 3) * 64 + (out_row >> 6) * 16 + (out_row & 1) * 8 + ((out_row >> 3) & 7)
    )
    turn_p[...] = jnp.where(in_row == source, 1.0, 0.0).astype(bf16)

    pl.semaphore_wait(barrier, CHIPS + 1)

    q_copies = {}
    for d in (4, 3, 5, 2, 6, 1, 7):
        dst = (chip + d) % CHIPS
        q_copies[d] = pltpu.make_async_remote_copy(
            src_ref=qslot.at[dst],
            dst_ref=qrecv.at[core, chip],
            send_sem=q_ss.at[d],
            recv_sem=q_rs.at[d],
            device_id=at_chip(dst),
            device_id_type=MESH,
        )
        q_copies[d].start()
    qrecv[core, chip] = qslot[chip]
    forwards = {}

    def forward(d):
        src = (chip + CHIPS - d) % CHIPS
        if d:
            q_copies[d].wait_recv()
        forwards[d] = pltpu.make_async_remote_copy(
            src_ref=qrecv.at[core, src],
            dst_ref=qrecv.at[core, src],
            send_sem=qf_ss.at[d],
            recv_sem=qf_rs.at[d],
            device_id=sibling,
            device_id_type=MESH,
        )
        forwards[d].start()

    forward(0)

    def split_heads(src, dst):
        def step(i, carry):
            first = pl.multiple_of(i * 512, 512)
            rows = jnp.concatenate(
                [src[pl.ds(first, 256), :], src[pl.ds(first + 256, 256), :]], axis=1
            )
            parted = jnp.dot(split_p[...], rows, preferred_element_type=f32).astype(bf16)
            to = pl.multiple_of(i * 64, 64)
            for k in range(8):
                dst[k, pl.ds(to, 32), :] = parted[k * 32 : (k + 1) * 32, :HD]
                dst[k, pl.ds(to + 32, 32), :] = parted[k * 32 : (k + 1) * 32, HD:]
            return carry

        lax.fori_loop(0, 8, step, 0)

    local_copies[0].wait()
    split_heads(pre, pkv)

    lkv[:, SUF:, :] = jnp.zeros((8, LOCAL - SUF, HD), bf16)
    col = lax.broadcasted_iota(jnp.int32, (ROWS, LOCAL), 1)
    step_of = lax.broadcasted_iota(jnp.int32, (ROWS, LOCAL), 0) // GROUP

    def local_part(s):
        local_copies[1 + s].wait()
        split_heads(suf.at[s], lkv)
        lkv[:, SUF : SUF + 16, :] = new_ref[s]
        limit = jnp.where(col < SUF, slen_ref[s], SUF + 1 + step_of)
        ok = col < limit
        for g in range(KVL):
            query = q_ref[s, g * ROWS : (g + 1) * ROWS, :]
            scores = lax.dot_general(query, lkv[g], NT, preferred_element_type=f32) * SCALE
            masked = jnp.where(ok, scores, -1e30)
            top = jnp.max(masked, axis=1, keepdims=True)
            weights = jnp.where(ok, jnp.exp(masked - top), 0.0)
            total = jnp.sum(weights, axis=1, keepdims=True)
            result = jnp.dot(weights.astype(bf16), lkv[KVL + g], preferred_element_type=f32)
            here = slice(g * ROWS, (g + 1) * ROWS)
            lo[s, here, :] = result
            lm[s, here, :] = jnp.broadcast_to(top, (ROWS, HD))
            ll[s, here, :] = jnp.broadcast_to(total, (ROWS, HD))

    local_part(0)
    forward(1)
    forward(7)
    local_part(1)
    forward(2)
    forward(6)
    local_part(2)
    for d in (3, 5, 4):
        forward(d)
    local_part(3)

    usable = lax.broadcasted_iota(jnp.int32, (256, PSH), 1) < prompt_rows - core * PSH

    def prefix_half(which):
        for g in range(KVL):
            query = qrecv[which, :, :, :].reshape(CHIPS, MOST, KVL, ROWS, HD)[:, :, g]
            query = query.reshape(256, HD)
            scores = lax.dot_general(query, pkv[g], NT, preferred_element_type=f32) * SCALE
            masked = jnp.where(usable, scores, -1e30)
            top = jnp.max(masked, axis=1, keepdims=True)
            weights = jnp.where(usable, jnp.exp(masked - top), 0.0)
            total = jnp.sum(weights, axis=1, keepdims=True)
            result = jnp.dot(weights.astype(bf16), pkv[KVL + g], preferred_element_type=f32)
            shape = (CHIPS, MOST, ROWS, HD)
            half_o[:, :, g] = result.reshape(shape)
            half_m[:, :, g] = jnp.broadcast_to(top, (256, HD)).reshape(shape)
            half_l[:, :, g] = jnp.broadcast_to(total, (256, HD)).reshape(shape)

    sub = lax.broadcasted_iota(jnp.int32, (8, HD), 0)

    def stat_rows(top, total):
        return jnp.where(sub == 0, top.T[:8], total.T[:8])

    for d in (0, 1, 2, 3, 4, 5, 6, 7):
        forwards[d].wait_recv()
    prefix_half(1 - core)

    def pack_half(c, carry):
        so_send[c] = half_o[c].reshape(128, HD).astype(bf16)
        st_send[c] = stat_rows(half_m[c].reshape(128, HD), half_l[c].reshape(128, HD))
        return carry

    lax.fori_loop(0, CHIPS, pack_half, 0)
    swaps = []
    for i, (src, dst) in enumerate(((so_send, so_recv), (st_send, st_recv))):
        copy = pltpu.make_async_remote_copy(
            src_ref=src,
            dst_ref=dst,
            send_sem=x_ss.at[i],
            recv_sem=x_rs.at[i],
            device_id=sibling,
            device_id_type=MESH,
        )
        copy.start()
        swaps.append(copy)
    prefix_half(core)
    for copy in swaps:
        copy.wait_recv()

    results = []

    def merge(c):
        m1, l1 = half_m[c].reshape(128, HD), half_l[c].reshape(128, HD)
        other = st_recv[c]
        m2 = jnp.broadcast_to(other[0:1], (HD, HD)).T
        l2 = jnp.broadcast_to(other[1:2], (HD, HD)).T
        top = jnp.maximum(m1, m2)
        w1, w2 = jnp.exp(m1 - top), jnp.exp(m2 - top)
        total = w1 * l1 + w2 * l2
        mixed = w1 * half_o[c].reshape(128, HD) + w2 * so_recv[c].astype(f32)
        return (mixed / total).astype(bf16), stat_rows(top, total)

    for d in (4, 3, 5, 2, 6, 1, 7):
        dst = (chip + d) % CHIPS
        co_send[dst], cs_send[dst] = merge(dst)
        for src, target, ss, rs in (
            (co_send, co_recv, c_ss, c_rs),
            (cs_send, cs_recv, s_ss, s_rs),
        ):
            copy = pltpu.make_async_remote_copy(
                src_ref=src.at[dst],
                dst_ref=target.at[chip],
                send_sem=ss.at[d],
                recv_sem=rs.at[d],
                device_id=at_chip(dst),
                device_id_type=MESH,
            )
            copy.start()
            results.append(copy)
    co_recv[chip], cs_recv[chip] = merge(chip)
    for copy in results:
        copy.wait_recv()

    parts = []
    for s in range(HELD):
        stats = cs_recv[groups[s]]
        block = co_recv[groups[s]].astype(f32)
        first = jnp.broadcast_to(ranks[s] == 0, (SPAN, HD))
        tops = jnp.broadcast_to(stats[0:1], (HD, HD)).T
        totals = jnp.broadcast_to(stats[1:2], (HD, HD)).T
        pm = jnp.where(first, tops[:SPAN], tops[SPAN:])
        pt = jnp.where(first, totals[:SPAN], totals[SPAN:])
        po = jnp.where(first, block[:SPAN], block[SPAN:])
        overall = jnp.maximum(pm, lm[s])
        wp = pt * jnp.exp(pm - overall)
        wl = jnp.exp(lm[s] - overall)
        parts.append(((wp * po + wl * lo[s]) / (wp + wl * ll[s])).astype(bf16))
    attn = jnp.concatenate(parts, axis=0)
    ag[wide] = jnp.dot(turn_p[...], attn, preferred_element_type=f32).astype(bf16)

    sends = []

    def push(index, ss, rs, device):
        copy = pltpu.make_async_remote_copy(
            src_ref=ag.at[index],
            dst_ref=ag.at[index],
            send_sem=ss,
            recv_sem=rs,
            device_id=device,
            device_id_type=MESH,
        )
        copy.start()
        sends.append(copy)
        return copy

    x_peer = at_chip(zc * 2 + 1 - xc)
    z_in = {}
    for d in (2, 1, 3):
        z_in[d] = push(wide, z_ss.at[d], z_rs.at[d], at_chip(((zc + d) % 4) * 2 + xc))
    x_in = {0: push(wide, ax_ss.at[0], ax_rs.at[0], x_peer)}
    c_in = [push(wide, ac_ss.at[0], ac_rs.at[0], sibling)]

    def pass_x(d):
        x_in[d].wait_recv()
        index = (((zc + 4 - d) % 4) * 2 + 1 - xc) * 2 + core
        c_in.append(push(index, ac_ss.at[4 + d], ac_rs.at[4 + d], sibling))

    def pass_z(d):
        z_in[d].wait_recv()
        index = (((zc + 4 - d) % 4) * 2 + xc) * 2 + core
        x_in[d] = push(index, ax_ss.at[d], ax_rs.at[d], x_peer)
        c_in.append(push(index, ac_ss.at[d], ac_rs.at[d], sibling))

    for d in (1, 3, 2):
        pass_z(d)
    for d in (0, 1, 3, 2):
        pass_x(d)
    local_copies[1 + HELD].wait()
    for copy in c_in:
        copy.wait_recv()

    for k in range(16):
        block = ag[:, k * 16 : (k + 1) * 16, :].astype(f32)
        lhs[:, k * 256 : k * 256 + 128] = block[:, :8].reshape(128, HD).astype(bf16)
        lhs[:, k * 256 + 128 : (k + 1) * 256] = block[:, 8:].reshape(128, HD).astype(bf16)

    theirs = pl.multiple_of((1 - y) * 64, 64)
    mine = pl.multiple_of(y * 64, 64)
    y_copies = []
    for n in range(2):
        terms[n] = jnp.dot(
            lhs[...], w[:, n * 256 : (n + 1) * 256], preferred_element_type=f32
        )
        y_send[n] = terms[n, pl.ds(theirs, 64), :].astype(bf16)
        copy = pltpu.make_async_remote_copy(
            src_ref=y_send.at[n],
            dst_ref=y_recv.at[n],
            send_sem=y_ss.at[n],
            recv_sem=y_rs.at[n],
            device_id=(wide, 1 - y),
            device_id_type=MESH,
        )
        copy.start()
        y_copies.append(copy)
    for n in range(2):
        y_copies[n].wait_recv()
        total = terms[n, pl.ds(mine, 64), :] + y_recv[n].astype(f32)
        o_ref[:, n * 256 : (n + 1) * 256] = total.astype(bf16)

    for copy in [*q_copies.values(), *forwards.values(), *swaps, *results, *sends, *y_copies]:
        copy.wait_send()


def fused_device(
    queries,
    new_kv,
    suffix_cache,
    suffix_len,
    prefix_cache,
    prompt_len,
    prompt_slot,
    sample_prompt,
    out_weight,
):
    f32, bf16 = jnp.float32, jnp.bfloat16
    q_rows = queries.reshape(HELD, STEPS, KVL, GROUP, HD).transpose(0, 2, 1, 3, 4)
    q_rows = q_rows.reshape(HELD, SPAN, HD)
    new_rows = new_kv.reshape(HELD, STEPS, KVL, 2, HD).transpose(0, 3, 2, 1, 4)
    new_rows = jnp.pad(
        new_rows.reshape(HELD, 2 * KVL, STEPS, HD), ((0, 0), (0, 0), (0, 16 - STEPS), (0, 0))
    )
    suf = suffix_cache.reshape(HELD, SUF, KVL, 2, HD).transpose(0, 1, 3, 2, 4)
    suf = suf.reshape(HELD, SUF * 8, HD)
    pre = prefix_cache.reshape(PSH, KVL, 2, HD).transpose(0, 2, 1, 3).reshape(PSH * 8, HD)
    vm, sm, hbm = pltpu.VMEM, pltpu.SMEM, pl.ANY
    dma = pltpu.SemaphoreType.DMA
    half = (CHIPS, MOST, KVL, ROWS, HD)
    scratch = [
        vm((HELD, SUF * 8, HD), bf16),
        vm((PSH * 8, HD), bf16),
        vm((KVL * 1024, 512), bf16),
        vm((256, 256), bf16),
        vm((256, 256), bf16),
        vm((8, LOCAL, HD), bf16),
        vm((8, PSH, HD), bf16),
        vm((CHIPS, 128, HD), bf16),
        vm((2, CHIPS, 128, HD), bf16),
        vm((HELD, SPAN, HD), f32),
        vm((HELD, SPAN, HD), f32),
        vm((HELD, SPAN, HD), f32),
        vm(half, f32),
        vm(half, f32),
        vm(half, f32),
        vm((CHIPS, 128, HD), bf16),
        vm((CHIPS, 8, HD), f32),
        vm((CHIPS, 128, HD), bf16),
        vm((CHIPS, 8, HD), f32),
        vm((CHIPS, 128, HD), bf16),
        vm((CHIPS, 8, HD), f32),
        vm((CHIPS, 128, HD), bf16),
        vm((CHIPS, 8, HD), f32),
        vm((16, 256, HD), bf16),
        vm((128, 4096), bf16),
        vm((2, 128, 256), f32),
        vm((2, 64, 256), bf16),
        vm((2, 64, 256), bf16),
        dma((2 + HELD,)),
    ]
    for count in (8, 8, 2, 8, 8, 4, 4, 8, 2):
        scratch += [dma((count,)), dma((count,))]
    out = pl.pallas_call(
        fused_kernel,
        out_shape=jax.ShapeDtypeStruct((64, 512), bf16),
        in_specs=[pl.BlockSpec(memory_space=sm)] * 4
        + [pl.BlockSpec(memory_space=vm)] * 2
        + [pl.BlockSpec(memory_space=hbm)] * 3,
        out_specs=pl.BlockSpec(memory_space=vm),
        scratch_shapes=scratch,
        compiler_params=pltpu.CompilerParams(
            collective_id=0, has_side_effects=True, vmem_limit_bytes=56 * 1024 * 1024
        ),
        cost_estimate=pl.CostEstimate(
            flops=4_000_000_000, bytes_accessed=12_000_000, transcendentals=1_500_000
        ),
    )(
        suffix_len,
        prompt_len,
        prompt_slot,
        sample_prompt.reshape(-1),
        q_rows,
        new_rows,
        suf,
        pre,
        out_weight,
    )
    return out.reshape(32, STEPS, 512)


def solution(mesh):
    small = mesh.shape["wide"] == 2 * CHIPS and mesh.shape["kv"] == 2
    return jax.shard_map(
        fused_device if small else general_device,
        mesh=mesh,
        in_specs=(
            P("wide", None, "kv"),
            P("wide", None, "kv", None),
            P("wide", None, "kv", None),
            P("wide"),
            P("wide", "kv", None),
            P(),
            P(),
            P(),
            P("kv", "wide"),
        ),
        out_specs=P("kv", None, "wide"),
        check_vma=False,
    )
```

```python
import functools
import math

import jax
import jax.numpy as jnp
from jax import lax
from jax.experimental import pallas as pl
from jax.experimental.pallas import tpu as pltpu
from jax.sharding import PartitionSpec as P

HD = 128
GROUP = 8
STEPS = 2
PSH = 512
SUF = 512
NPROMPT = 8
MOST = 2


def sample_ranks(prompt_block):
    length = prompt_block.shape[-1]
    earlier = jnp.arange(length)[None, :] < jnp.arange(length)[:, None]
    matching = prompt_block[..., :, None] == prompt_block[..., None, :]
    return jnp.sum(matching & earlier, axis=-1)


def prefix_part(slots, prefix_cache, prompt_rows, segment):
    sources = slots.shape[0]
    item_count = slots.shape[1]
    kv_local = prefix_cache.shape[1]
    batch_rows = sources * item_count * STEPS
    scale = HD ** (-0.5)
    key_rows = prefix_cache[:, :, :HD]
    value_rows = prefix_cache[:, :, HD:]
    usable = segment * PSH + jnp.arange(PSH) < prompt_rows
    block_rows = math.gcd(batch_rows, max(1, 512 // (kv_local * GROUP)))

    def one_block(query_block):
        scores = (
            jnp.einsum("bgxd,jgd->bgxj", query_block, key_rows, preferred_element_type=jnp.float32)
            * scale
        )
        masked = jnp.where(usable, scores, -1e30)
        row_max = jnp.max(masked, axis=-1)
        weights = jnp.where(usable, jnp.exp(masked - row_max[..., None]), 0.0)
        row_sum = jnp.sum(weights, axis=-1)
        weights_bf = (weights / jnp.maximum(row_sum, 1.0)[..., None]).astype(jnp.bfloat16)
        result = jnp.einsum(
            "bgxj,jgd->bgxd", weights_bf, value_rows, preferred_element_type=jnp.float32
        )
        return (result.astype(jnp.bfloat16), row_max, row_sum)

    query_blocks = slots.reshape(batch_rows // block_rows, block_rows, kv_local, GROUP, HD)
    results = lax.map(one_block, query_blocks)
    part_out = results[0].reshape(sources, item_count, -1)
    part_max = results[1].reshape(sources, item_count, -1)
    part_sum = results[2].reshape(sources, item_count, -1)
    part_out = lax.all_to_all(part_out, "wide", split_axis=0, concat_axis=0, tiled=True)
    part_max, part_sum = (
        lax.all_to_all(part_max, "wide", split_axis=0, concat_axis=0, tiled=True),
        lax.all_to_all(part_sum, "wide", split_axis=0, concat_axis=0, tiled=True),
    )
    return (part_out, part_max, part_sum)


def general_device(
    queries,
    new_kv,
    suffix_cache,
    suffix_len,
    prefix_cache,
    prompt_len,
    prompt_slot,
    sample_prompt,
    out_weight,
):
    wide_count = lax.axis_size("wide")
    split_count = wide_count // NPROMPT
    position = lax.axis_index("wide")
    held_rows = queries.shape[0]
    kv_local = new_kv.shape[2]
    scale = HD ** (-0.5)
    prompt_ids = sample_prompt[:, 0]
    my_prompts = lax.dynamic_slice_in_dim(prompt_ids, position * held_rows, held_rows)
    prompt_range = jnp.arange(NPROMPT)
    slot_range = jnp.arange(MOST)
    my_group = jnp.sum(
        jnp.where(my_prompts[:, None] == prompt_range[None, :], prompt_slot[None, :], 0), axis=1
    )
    my_rank = sample_ranks(my_prompts)
    picked = (my_group[:, None, None] == prompt_range[None, :, None]) & (
        my_rank[:, None, None] == slot_range[None, None, :]
    )
    own_group = position // split_count
    segment = position % split_count
    owner_match = prompt_slot == own_group
    prompt_rows = jnp.sum(jnp.where(owner_match, prompt_len, 0))
    own_prompt = jnp.sum(jnp.where(owner_match, prompt_range, 0))
    flat_queries = queries.reshape(held_rows, -1)
    everyone = lax.all_gather(flat_queries, "wide", axis=0, tiled=True)
    blocks = prompt_ids.reshape(wide_count, held_rows)
    block_rank = sample_ranks(blocks)
    chosen = (blocks[:, :, None] == own_prompt) & (
        block_rank[:, :, None] == slot_range[None, None, :]
    )
    incoming = jnp.einsum(
        "hrc,hrx->hcx",
        chosen.astype(jnp.bfloat16),
        everyone.reshape(wide_count, held_rows, -1),
        preferred_element_type=jnp.float32,
    ).astype(jnp.bfloat16)
    part_out, part_max, part_sum = prefix_part(incoming, prefix_cache, prompt_rows, segment)
    picked_bf = picked.astype(jnp.bfloat16)
    picked_f32 = picked.astype(jnp.float32)
    prefix_out = jnp.einsum(
        "rgc,gscx->rsx",
        picked_bf,
        part_out.reshape(NPROMPT, split_count, MOST, -1),
        preferred_element_type=jnp.float32,
    )
    prefix_max = jnp.einsum(
        "rgc,gscy->rsy",
        picked_f32,
        part_max.reshape(NPROMPT, split_count, MOST, -1),
        precision=lax.Precision.HIGHEST,
    )
    prefix_sum = jnp.einsum(
        "rgc,gscy->rsy",
        picked_f32,
        part_sum.reshape(NPROMPT, split_count, MOST, -1),
        precision=lax.Precision.HIGHEST,
    )
    prefix_out = prefix_out.reshape(held_rows, split_count, STEPS, kv_local, GROUP, HD)
    prefix_max = prefix_max.reshape(held_rows, split_count, STEPS, kv_local, GROUP)
    prefix_sum = prefix_sum.reshape(held_rows, split_count, STEPS, kv_local, GROUP)
    query_rows = queries.reshape(held_rows, STEPS, kv_local, GROUP, HD)
    local_rows = jnp.concatenate([suffix_cache, new_kv], axis=1)
    local_scores = (
        jnp.einsum(
            "stgxd,sjgd->stgxj",
            query_rows,
            local_rows[..., :HD],
            preferred_element_type=jnp.float32,
        )
        * scale
    )
    positions = jnp.arange(SUF + STEPS)
    step_ids = jnp.arange(STEPS)
    local_ok = jnp.where(
        positions[None, None, :] < SUF,
        positions[None, None, :] < suffix_len[:, None, None],
        positions[None, None, :] - SUF <= step_ids[None, :, None],
    )
    local_ok = local_ok[:, :, None, None, :]
    local_masked = jnp.where(local_ok, local_scores, -1e30)
    local_max = jnp.max(local_masked, axis=-1)
    local_weights = jnp.where(local_ok, jnp.exp(local_masked - local_max[..., None]), 0.0)
    local_sum = jnp.sum(local_weights, axis=-1)
    local_bf = (local_weights / local_sum[..., None]).astype(jnp.bfloat16)
    local_out = jnp.einsum(
        "stgxj,sjgd->stgxd", local_bf, local_rows[..., HD:], preferred_element_type=jnp.float32
    )
    overall = jnp.maximum(jnp.max(prefix_max, axis=1), local_max)
    seg_weight = prefix_sum * jnp.exp(prefix_max - overall[:, None])
    local_weight = local_sum * jnp.exp(local_max - overall)
    numerator = (
        jnp.sum(seg_weight[..., None] * prefix_out, axis=1) + local_weight[..., None] * local_out
    )
    denominator = jnp.sum(seg_weight, axis=1) + local_weight
    attn = (numerator / denominator[..., None]).astype(jnp.bfloat16).reshape(held_rows, STEPS, -1)
    terms = jnp.einsum(
        "stk,kd->std",
        lax.all_gather(attn, "wide", axis=0, tiled=True),
        out_weight,
        preferred_element_type=jnp.float32,
    )
    summed = lax.psum_scatter(terms, "kv", scatter_dimension=0, tiled=True)
    return summed.astype(jnp.bfloat16)


MESH = pl.DeviceIdType.MESH
CHIPS = 8
HELD = 4
KVL = 4
ROWS = STEPS * GROUP
SPAN = KVL * ROWS
SUF_ROWS = SUF * 2 * KVL
LOCAL = SUF_ROWS + 128
FAR = 1 << 20
SCALE2 = HD ** (-0.5) * math.log2(math.e)
NT = (((1,), (1,)), ((), ()))


def fused_kernel(
    slen_ref,
    plen_ref,
    pslot_ref,
    sprompt_ref,
    q_ref,
    new_ref,
    suf_hbm,
    pre_hbm,
    w_hbm,
    o_ref,
    suf,
    pre,
    w,
    split_p,
    turn_p,
    place,
    pkv,
    qslot,
    qrecv,
    lo,
    lm,
    ll,
    half_o,
    half_m,
    half_l,
    so_send,
    st_send,
    so_recv,
    st_recv,
    co_send,
    cs_send,
    co_recv,
    cs_recv,
    ag,
    lhs,
    terms,
    y_send,
    y_recv,
    loc_sem,
    q_ss,
    q_rs,
    qf_ss,
    qf_rs,
    x_ss,
    x_rs,
    c_ss,
    c_rs,
    s_ss,
    s_rs,
    z_ss,
    z_rs,
    ax_ss,
    ax_rs,
    ac_ss,
    ac_rs,
    y_ss,
    y_rs,
):
    f32, bf16 = jnp.float32, jnp.bfloat16
    wide = lax.axis_index("wide")
    y = lax.axis_index("kv")
    chip = wide // 2
    core = wide % 2
    zc = chip // 2
    xc = chip % 2
    sibling = (chip * 2 + 1 - core, y)

    def at_chip(c):
        return (c * 2 + core, y)

    local_copies = [pltpu.make_async_copy(pre_hbm, pre, loc_sem.at[0])]
    local_copies += [
        pltpu.make_async_copy(
            suf_hbm.at[s], suf.at[s, pl.ds(0, SUF_ROWS)], loc_sem.at[1 + s]
        ) for s in range(HELD)
    ]
    local_copies.append(pltpu.make_async_copy(w_hbm, w, loc_sem.at[1 + HELD]))
    for copy in local_copies:
        copy.start()

    barrier = pltpu.get_barrier_semaphore()
    for d in range(1, CHIPS):
        pl.semaphore_signal(
            barrier, inc=1, device_id=at_chip((chip + d) % CHIPS), device_id_type=MESH
        )
    pl.semaphore_signal(barrier, inc=1, device_id=sibling, device_id_type=MESH)
    pl.semaphore_signal(barrier, inc=1, device_id=(wide, 1 - y), device_id_type=MESH)

    prompts = [sprompt_ref[wide * HELD + s] for s in range(HELD)]
    groups = [pslot_ref[p] for p in prompts]
    ranks = []
    for s in range(HELD):
        rank = jnp.int32(0)
        for e in range(s):
            rank = rank + jnp.where(prompts[e] == prompts[s], 1, 0)
        ranks.append(rank)
    for c in range(CHIPS):
        for m in range(MOST):
            pick = jnp.int32(0)
            for s in range(1, HELD):
                pick = pick + jnp.where((groups[s] == c) & (ranks[s] == m), s, 0)
            qslot[c, m * SPAN : (m + 1) * SPAN, :] = q_ref[pick]
    prompt_rows = jnp.int32(0)
    for p in range(NPROMPT):
        prompt_rows = prompt_rows + jnp.where(pslot_ref[p] == chip, plen_ref[p], 0)

    out_row = lax.broadcasted_iota(jnp.int32, (256, 256), 0)
    in_row = lax.broadcasted_iota(jnp.int32, (256, 256), 1)
    split_p[...] = jnp.where(in_row == (out_row & 31) * 8 + (out_row >> 5), 1.0, 0.0).astype(bf16)
    source = (
        ((out_row >> 1) & 3) * 64 + (out_row >> 6) * 16 + (out_row & 1) * 8 + ((out_row >> 3) & 7)
    )
    turn_p[...] = jnp.where(in_row == source, 1.0, 0.0).astype(bf16)

    pl.semaphore_wait(barrier, CHIPS + 1)

    q_copies = {}
    for d in (4, 3, 5, 2, 6, 1, 7):
        dst = (chip + d) % CHIPS
        q_copies[d] = pltpu.make_async_remote_copy(
            src_ref=qslot.at[dst],
            dst_ref=qrecv.at[core, chip],
            send_sem=q_ss.at[d],
            recv_sem=q_rs.at[d],
            device_id=at_chip(dst),
            device_id_type=MESH,
        )
        q_copies[d].start()
    qrecv[core, chip] = qslot[chip]
    forwards = {}

    def forward(d):
        src = (chip + CHIPS - d) % CHIPS
        if d:
            q_copies[d].wait_recv()
        forwards[d] = pltpu.make_async_remote_copy(
            src_ref=qrecv.at[core, src],
            dst_ref=qrecv.at[core, src],
            send_sem=qf_ss.at[d],
            recv_sem=qf_rs.at[d],
            device_id=sibling,
            device_id_type=MESH,
        )
        forwards[d].start()

    forward(0)

    local_copies[0].wait()
    for i in range(8):
        rows = jnp.concatenate(
            [pre[i * 512 : i * 512 + 256, :], pre[i * 512 + 256 : (i + 1) * 512, :]], axis=1
        )
        parted = jnp.dot(split_p[...], rows, preferred_element_type=f32).astype(bf16)
        for k in range(8):
            pkv[k, i * 64 : i * 64 + 32, :] = parted[k * 32 : (k + 1) * 32, :HD]
            pkv[k, i * 64 + 32 : (i + 1) * 64, :] = parted[k * 32 : (k + 1) * 32, HD:]

    col = lax.broadcasted_iota(jnp.int32, (SPAN, LOCAL), 1)
    row = lax.broadcasted_iota(jnp.int32, (SPAN, LOCAL), 0)
    spot = col >> 3
    fresh = jnp.where(spot - SUF <= ((row >> 3) & 1), -1, FAR)
    place[...] = jnp.where((col & 7) == (row >> 4), jnp.where(spot < SUF, spot, fresh), FAR)

    def local_part(s):
        local_copies[1 + s].wait()
        suf[s, SUF_ROWS : SUF_ROWS + 16, :] = new_ref[s]
        suf[s, SUF_ROWS + 16 :, :] = jnp.zeros((LOCAL - SUF_ROWS - 16, HD), bf16)
        scores = lax.dot_general(q_ref[s], suf[s], NT, preferred_element_type=f32)
        masked = jnp.where(place[...] < slen_ref[s], scores * SCALE2, -1e30)
        top = jnp.max(masked, axis=1, keepdims=True)
        weights = jnp.exp2(masked - top)
        total = jnp.sum(weights, axis=1, keepdims=True)
        moved = pltpu.roll(weights, KVL, 1).astype(bf16)
        lo[s] = jnp.dot(moved, suf[s], preferred_element_type=f32)
        lm[s] = jnp.broadcast_to(top, (SPAN, HD))
        ll[s] = jnp.broadcast_to(total, (SPAN, HD))

    local_part(0)
    forward(1)
    forward(7)
    local_part(1)
    for d in (2, 6, 3, 5, 4):
        forward(d)

    usable = lax.broadcasted_iota(jnp.int32, (256, PSH), 1) < prompt_rows - core * PSH

    def prefix_half(which):
        for g in range(KVL):
            query = qrecv[which, :, :, :].reshape(CHIPS, MOST, KVL, ROWS, HD)[:, :, g]
            query = query.reshape(256, HD)
            scores = lax.dot_general(query, pkv[g], NT, preferred_element_type=f32)
            masked = jnp.where(usable, scores * SCALE2, -1e30)
            top = jnp.max(masked, axis=1, keepdims=True)
            weights = jnp.exp2(masked - top)
            total = jnp.sum(weights, axis=1, keepdims=True)
            result = jnp.dot(weights.astype(bf16), pkv[KVL + g], preferred_element_type=f32)
            shape = (CHIPS, MOST, ROWS, HD)
            half_o[:, :, g] = result.reshape(shape)
            half_m[:, :, g] = jnp.broadcast_to(top, (256, HD)).reshape(shape)
            half_l[:, :, g] = jnp.broadcast_to(total, (256, HD)).reshape(shape)

    sub = lax.broadcasted_iota(jnp.int32, (8, HD), 0)

    def stat_rows(top, total):
        return jnp.where(sub == 0, top.T[:8], total.T[:8])

    for d in (0, 1, 2, 3, 4, 5, 6, 7):
        forwards[d].wait_recv()
    prefix_half(1 - core)

    def pack_half(c, carry):
        so_send[c] = half_o[c].reshape(128, HD).astype(bf16)
        st_send[c] = stat_rows(half_m[c].reshape(128, HD), half_l[c].reshape(128, HD))
        return carry

    lax.fori_loop(0, CHIPS, pack_half, 0)
    swaps = []
    for i, (src, dst) in enumerate(((so_send, so_recv), (st_send, st_recv))):
        copy = pltpu.make_async_remote_copy(
            src_ref=src,
            dst_ref=dst,
            send_sem=x_ss.at[i],
            recv_sem=x_rs.at[i],
            device_id=sibling,
            device_id_type=MESH,
        )
        copy.start()
        swaps.append(copy)
    prefix_half(core)
    for copy in swaps:
        copy.wait_recv()

    results = []

    def merge(c):
        m1, l1 = half_m[c].reshape(128, HD), half_l[c].reshape(128, HD)
        other = st_recv[c]
        m2 = jnp.broadcast_to(other[0:1], (HD, HD)).T
        l2 = jnp.broadcast_to(other[1:2], (HD, HD)).T
        top = jnp.maximum(m1, m2)
        w1, w2 = jnp.exp2(m1 - top), jnp.exp2(m2 - top)
        total = w1 * l1 + w2 * l2
        mixed = w1 * half_o[c].reshape(128, HD) + w2 * so_recv[c].astype(f32)
        return (mixed / total).astype(bf16), stat_rows(top, total)

    for d in (4, 3, 5, 2, 6, 1, 7):
        dst = (chip + d) % CHIPS
        co_send[dst], cs_send[dst] = merge(dst)
        for src, target, ss, rs in (
            (co_send, co_recv, c_ss, c_rs),
            (cs_send, cs_recv, s_ss, s_rs),
        ):
            copy = pltpu.make_async_remote_copy(
                src_ref=src.at[dst],
                dst_ref=target.at[chip],
                send_sem=ss.at[d],
                recv_sem=rs.at[d],
                device_id=at_chip(dst),
                device_id_type=MESH,
            )
            copy.start()
            results.append(copy)
    co_recv[chip], cs_recv[chip] = merge(chip)
    local_part(2)
    local_part(3)
    for copy in results:
        copy.wait_recv()

    parts = []
    for s in range(HELD):
        stats = cs_recv[groups[s]]
        block = co_recv[groups[s]].astype(f32)
        first = jnp.broadcast_to(ranks[s] == 0, (SPAN, HD))
        tops = jnp.broadcast_to(stats[0:1], (HD, HD)).T
        totals = jnp.broadcast_to(stats[1:2], (HD, HD)).T
        pm = jnp.where(first, tops[:SPAN], tops[SPAN:])
        pt = jnp.where(first, totals[:SPAN], totals[SPAN:])
        po = jnp.where(first, block[:SPAN], block[SPAN:])
        overall = jnp.maximum(pm, lm[s])
        wp = pt * jnp.exp2(pm - overall)
        wl = jnp.exp2(lm[s] - overall)
        parts.append(((wp * po + wl * lo[s]) / (wp + wl * ll[s])).astype(bf16))
    attn = jnp.concatenate(parts, axis=0)
    turned = jnp.dot(turn_p[...], attn, preferred_element_type=f32).astype(bf16)
    ag[0, wide] = turned[:128]
    ag[1, wide] = turned[128:]

    sends = []

    def push(index, ss, rs, i, device):
        copy = pltpu.make_async_remote_copy(
            src_ref=ag.at[index],
            dst_ref=ag.at[index],
            send_sem=ss.at[i],
            recv_sem=rs.at[i],
            device_id=device,
            device_id_type=MESH,
        )
        copy.start()
        sends.append(copy)
        return copy

    x_peer = at_chip(zc * 2 + 1 - xc)
    z_in, x_in, c_in = {}, {}, ([], [])
    for h in range(2):
        x_in[h, 0] = push((h, wide), ax_ss, ax_rs, 4 * h, x_peer)
        for d in (2, 1, 3):
            device = at_chip(((zc + d) % 4) * 2 + xc)
            z_in[h, d] = push((h, wide), z_ss, z_rs, 4 * h + d, device)
        c_in[h].append(push((h, wide), ac_ss, ac_rs, 8 * h, sibling))

    def pass_x(h, d):
        x_in[h, d].wait_recv()
        index = (((zc + 4 - d) % 4) * 2 + 1 - xc) * 2 + core
        c_in[h].append(push((h, index), ac_ss, ac_rs, 8 * h + 4 + d, sibling))

    def pass_z(h, d):
        z_in[h, d].wait_recv()
        index = (((zc + 4 - d) % 4) * 2 + xc) * 2 + core
        x_in[h, d] = push((h, index), ax_ss, ax_rs, 4 * h + d, x_peer)
        c_in[h].append(push((h, index), ac_ss, ac_rs, 8 * h + d, sibling))

    def gather_rows(h):
        for copy in c_in[h]:
            copy.wait_recv()
        for k in range(8):
            block = ag[h, :, k * 16 : (k + 1) * 16, :].astype(f32)
            to = h * 2048 + k * 256
            lhs[:, to : to + 128] = block[:, :8].reshape(128, HD).astype(bf16)
            lhs[:, to + 128 : to + 256] = block[:, 8:].reshape(128, HD).astype(bf16)

    for d in (1, 3, 2):
        pass_z(0, d)
    for d in (0, 1, 3, 2):
        pass_x(0, d)
    for d in (1, 3, 2):
        pass_z(1, d)
    local_copies[1 + HELD].wait()
    gather_rows(0)
    for n in range(2):
        terms[n] = jnp.dot(
            lhs[:, :2048], w[:2048, n * 256 : (n + 1) * 256], preferred_element_type=f32
        )
    for d in (0, 1, 3, 2):
        pass_x(1, d)
    gather_rows(1)

    theirs = pl.multiple_of((1 - y) * 64, 64)
    mine = pl.multiple_of(y * 64, 64)
    y_copies = []
    for n in range(2):
        terms[n] += jnp.dot(
            lhs[:, 2048:], w[2048:, n * 256 : (n + 1) * 256], preferred_element_type=f32
        )
        y_send[n] = terms[n, pl.ds(theirs, 64), :].astype(bf16)
        copy = pltpu.make_async_remote_copy(
            src_ref=y_send.at[n],
            dst_ref=y_recv.at[n],
            send_sem=y_ss.at[n],
            recv_sem=y_rs.at[n],
            device_id=(wide, 1 - y),
            device_id_type=MESH,
        )
        copy.start()
        y_copies.append(copy)
    for n in range(2):
        y_copies[n].wait_recv()
        total = terms[n, pl.ds(mine, 64), :] + y_recv[n].astype(f32)
        o_ref[:, n * 256 : (n + 1) * 256] = total.astype(bf16)

    for copy in [*q_copies.values(), *forwards.values(), *swaps, *results, *sends, *y_copies]:
        copy.wait_send()


def fused_device(
    queries,
    new_kv,
    suffix_cache,
    suffix_len,
    prefix_cache,
    prompt_len,
    prompt_slot,
    sample_prompt,
    out_weight,
):
    f32, bf16 = jnp.float32, jnp.bfloat16
    q_rows = queries.reshape(HELD, STEPS, KVL, GROUP, HD).transpose(0, 2, 1, 3, 4)
    q_rows = q_rows.reshape(HELD, SPAN, HD)
    new_rows = new_kv.reshape(HELD, STEPS, KVL, 2, HD).transpose(0, 1, 3, 2, 4)
    new_rows = new_rows.reshape(HELD, STEPS * 8, HD)
    suf = suffix_cache.reshape(HELD, SUF, KVL, 2, HD).transpose(0, 1, 3, 2, 4)
    suf = suf.reshape(HELD, SUF * 8, HD)
    pre = prefix_cache.reshape(PSH, KVL, 2, HD).transpose(0, 2, 1, 3).reshape(PSH * 8, HD)
    vm, sm, hbm = pltpu.VMEM, pltpu.SMEM, pl.ANY
    dma = pltpu.SemaphoreType.DMA
    half = (CHIPS, MOST, KVL, ROWS, HD)
    scratch = [
        vm((HELD, LOCAL, HD), bf16),
        vm((PSH * 8, HD), bf16),
        vm((KVL * 1024, 512), bf16),
        vm((256, 256), bf16),
        vm((256, 256), bf16),
        vm((SPAN, LOCAL), jnp.int32),
        vm((8, PSH, HD), bf16),
        vm((CHIPS, 128, HD), bf16),
        vm((2, CHIPS, 128, HD), bf16),
        vm((HELD, SPAN, HD), f32),
        vm((HELD, SPAN, HD), f32),
        vm((HELD, SPAN, HD), f32),
        vm(half, f32),
        vm(half, f32),
        vm(half, f32),
        vm((CHIPS, 128, HD), bf16),
        vm((CHIPS, 8, HD), f32),
        vm((CHIPS, 128, HD), bf16),
        vm((CHIPS, 8, HD), f32),
        vm((CHIPS, 128, HD), bf16),
        vm((CHIPS, 8, HD), f32),
        vm((CHIPS, 128, HD), bf16),
        vm((CHIPS, 8, HD), f32),
        vm((2, 16, 128, HD), bf16),
        vm((128, 4096), bf16),
        vm((2, 128, 256), f32),
        vm((2, 64, 256), bf16),
        vm((2, 64, 256), bf16),
        dma((2 + HELD,)),
    ]
    for count in (8, 8, 2, 8, 8, 8, 8, 16, 2):
        scratch += [dma((count,)), dma((count,))]
    out = pl.pallas_call(
        fused_kernel,
        out_shape=jax.ShapeDtypeStruct((64, 512), bf16),
        in_specs=[pl.BlockSpec(memory_space=sm)] * 4
        + [pl.BlockSpec(memory_space=vm)] * 2
        + [pl.BlockSpec(memory_space=hbm)] * 3,
        out_specs=pl.BlockSpec(memory_space=vm),
        scratch_shapes=scratch,
        compiler_params=pltpu.CompilerParams(
            collective_id=0, has_side_effects=True, vmem_limit_bytes=56 * 1024 * 1024
        ),
        cost_estimate=pl.CostEstimate(
            flops=4_000_000_000, bytes_accessed=12_000_000, transcendentals=1_500_000
        ),
    )(
        suffix_len,
        prompt_len,
        prompt_slot,
        sample_prompt.reshape(-1),
        q_rows,
        new_rows,
        suf,
        pre,
        out_weight,
    )
    return out.reshape(32, STEPS, 512)


def solution(mesh):
    small = mesh.shape["wide"] == 2 * CHIPS and mesh.shape["kv"] == 2
    return jax.shard_map(
        fused_device if small else general_device,
        mesh=mesh,
        in_specs=(
            P("wide", None, "kv"),
            P("wide", None, "kv", None),
            P("wide", None, "kv", None),
            P("wide"),
            P("wide", "kv", None),
            P(),
            P(),
            P(),
            P("kv", "wide"),
        ),
        out_specs=P("kv", None, "wide"),
        check_vma=False,
    )
```

```python
import functools
import math

import jax
import jax.numpy as jnp
from jax import lax
from jax.experimental import pallas as pl
from jax.experimental.pallas import tpu as pltpu
from jax.sharding import PartitionSpec as P

HD = 128
GROUP = 8
STEPS = 2
PSH = 512
SUF = 512
NPROMPT = 8
MOST = 2


def sample_ranks(prompt_block):
    length = prompt_block.shape[-1]
    earlier = jnp.arange(length)[None, :] < jnp.arange(length)[:, None]
    matching = prompt_block[..., :, None] == prompt_block[..., None, :]
    return jnp.sum(matching & earlier, axis=-1)


def prefix_part(slots, prefix_cache, prompt_rows, segment):
    sources = slots.shape[0]
    item_count = slots.shape[1]
    kv_local = prefix_cache.shape[1]
    batch_rows = sources * item_count * STEPS
    scale = HD ** (-0.5)
    key_rows = prefix_cache[:, :, :HD]
    value_rows = prefix_cache[:, :, HD:]
    usable = segment * PSH + jnp.arange(PSH) < prompt_rows
    block_rows = math.gcd(batch_rows, max(1, 512 // (kv_local * GROUP)))

    def one_block(query_block):
        scores = (
            jnp.einsum("bgxd,jgd->bgxj", query_block, key_rows, preferred_element_type=jnp.float32)
            * scale
        )
        masked = jnp.where(usable, scores, -1e30)
        row_max = jnp.max(masked, axis=-1)
        weights = jnp.where(usable, jnp.exp(masked - row_max[..., None]), 0.0)
        row_sum = jnp.sum(weights, axis=-1)
        weights_bf = (weights / jnp.maximum(row_sum, 1.0)[..., None]).astype(jnp.bfloat16)
        result = jnp.einsum(
            "bgxj,jgd->bgxd", weights_bf, value_rows, preferred_element_type=jnp.float32
        )
        return (result.astype(jnp.bfloat16), row_max, row_sum)

    query_blocks = slots.reshape(batch_rows // block_rows, block_rows, kv_local, GROUP, HD)
    results = lax.map(one_block, query_blocks)
    part_out = results[0].reshape(sources, item_count, -1)
    part_max = results[1].reshape(sources, item_count, -1)
    part_sum = results[2].reshape(sources, item_count, -1)
    part_out = lax.all_to_all(part_out, "wide", split_axis=0, concat_axis=0, tiled=True)
    part_max, part_sum = (
        lax.all_to_all(part_max, "wide", split_axis=0, concat_axis=0, tiled=True),
        lax.all_to_all(part_sum, "wide", split_axis=0, concat_axis=0, tiled=True),
    )
    return (part_out, part_max, part_sum)


def general_device(
    queries,
    new_kv,
    suffix_cache,
    suffix_len,
    prefix_cache,
    prompt_len,
    prompt_slot,
    sample_prompt,
    out_weight,
):
    wide_count = lax.axis_size("wide")
    split_count = wide_count // NPROMPT
    position = lax.axis_index("wide")
    held_rows = queries.shape[0]
    kv_local = new_kv.shape[2]
    scale = HD ** (-0.5)
    prompt_ids = sample_prompt[:, 0]
    my_prompts = lax.dynamic_slice_in_dim(prompt_ids, position * held_rows, held_rows)
    prompt_range = jnp.arange(NPROMPT)
    slot_range = jnp.arange(MOST)
    my_group = jnp.sum(
        jnp.where(my_prompts[:, None] == prompt_range[None, :], prompt_slot[None, :], 0), axis=1
    )
    my_rank = sample_ranks(my_prompts)
    picked = (my_group[:, None, None] == prompt_range[None, :, None]) & (
        my_rank[:, None, None] == slot_range[None, None, :]
    )
    own_group = position // split_count
    segment = position % split_count
    owner_match = prompt_slot == own_group
    prompt_rows = jnp.sum(jnp.where(owner_match, prompt_len, 0))
    own_prompt = jnp.sum(jnp.where(owner_match, prompt_range, 0))
    flat_queries = queries.reshape(held_rows, -1)
    everyone = lax.all_gather(flat_queries, "wide", axis=0, tiled=True)
    blocks = prompt_ids.reshape(wide_count, held_rows)
    block_rank = sample_ranks(blocks)
    chosen = (blocks[:, :, None] == own_prompt) & (
        block_rank[:, :, None] == slot_range[None, None, :]
    )
    incoming = jnp.einsum(
        "hrc,hrx->hcx",
        chosen.astype(jnp.bfloat16),
        everyone.reshape(wide_count, held_rows, -1),
        preferred_element_type=jnp.float32,
    ).astype(jnp.bfloat16)
    part_out, part_max, part_sum = prefix_part(incoming, prefix_cache, prompt_rows, segment)
    picked_bf = picked.astype(jnp.bfloat16)
    picked_f32 = picked.astype(jnp.float32)
    prefix_out = jnp.einsum(
        "rgc,gscx->rsx",
        picked_bf,
        part_out.reshape(NPROMPT, split_count, MOST, -1),
        preferred_element_type=jnp.float32,
    )
    prefix_max = jnp.einsum(
        "rgc,gscy->rsy",
        picked_f32,
        part_max.reshape(NPROMPT, split_count, MOST, -1),
        precision=lax.Precision.HIGHEST,
    )
    prefix_sum = jnp.einsum(
        "rgc,gscy->rsy",
        picked_f32,
        part_sum.reshape(NPROMPT, split_count, MOST, -1),
        precision=lax.Precision.HIGHEST,
    )
    prefix_out = prefix_out.reshape(held_rows, split_count, STEPS, kv_local, GROUP, HD)
    prefix_max = prefix_max.reshape(held_rows, split_count, STEPS, kv_local, GROUP)
    prefix_sum = prefix_sum.reshape(held_rows, split_count, STEPS, kv_local, GROUP)
    query_rows = queries.reshape(held_rows, STEPS, kv_local, GROUP, HD)
    local_rows = jnp.concatenate([suffix_cache, new_kv], axis=1)
    local_scores = (
        jnp.einsum(
            "stgxd,sjgd->stgxj",
            query_rows,
            local_rows[..., :HD],
            preferred_element_type=jnp.float32,
        )
        * scale
    )
    positions = jnp.arange(SUF + STEPS)
    step_ids = jnp.arange(STEPS)
    local_ok = jnp.where(
        positions[None, None, :] < SUF,
        positions[None, None, :] < suffix_len[:, None, None],
        positions[None, None, :] - SUF <= step_ids[None, :, None],
    )
    local_ok = local_ok[:, :, None, None, :]
    local_masked = jnp.where(local_ok, local_scores, -1e30)
    local_max = jnp.max(local_masked, axis=-1)
    local_weights = jnp.where(local_ok, jnp.exp(local_masked - local_max[..., None]), 0.0)
    local_sum = jnp.sum(local_weights, axis=-1)
    local_bf = (local_weights / local_sum[..., None]).astype(jnp.bfloat16)
    local_out = jnp.einsum(
        "stgxj,sjgd->stgxd", local_bf, local_rows[..., HD:], preferred_element_type=jnp.float32
    )
    overall = jnp.maximum(jnp.max(prefix_max, axis=1), local_max)
    seg_weight = prefix_sum * jnp.exp(prefix_max - overall[:, None])
    local_weight = local_sum * jnp.exp(local_max - overall)
    numerator = (
        jnp.sum(seg_weight[..., None] * prefix_out, axis=1) + local_weight[..., None] * local_out
    )
    denominator = jnp.sum(seg_weight, axis=1) + local_weight
    attn = (numerator / denominator[..., None]).astype(jnp.bfloat16).reshape(held_rows, STEPS, -1)
    terms = jnp.einsum(
        "stk,kd->std",
        lax.all_gather(attn, "wide", axis=0, tiled=True),
        out_weight,
        preferred_element_type=jnp.float32,
    )
    summed = lax.psum_scatter(terms, "kv", scatter_dimension=0, tiled=True)
    return summed.astype(jnp.bfloat16)


MESH = pl.DeviceIdType.MESH
CHIPS = 8
HELD = 4
KVL = 4
ROWS = STEPS * GROUP
SPAN = KVL * ROWS
PART = SPAN // 2
PAIR = MOST * PART
SUF_ROWS = SUF * 2 * KVL
LOCAL = SUF_ROWS + 128
FAR = 1 << 20
SCALE2 = HD ** (-0.5) * math.log2(math.e)
NT = (((1,), (1,)), ((), ()))


def fused_kernel(
    slen_ref,
    plen_ref,
    pslot_ref,
    sprompt_ref,
    q_ref,
    new_ref,
    suf_hbm,
    pre_hbm,
    w_hbm,
    o_ref,
    suf,
    pre,
    w,
    split_p,
    turn_p,
    out_p,
    place,
    pkv,
    qslot,
    qrecv,
    lo,
    lm,
    ll,
    half_o,
    half_m,
    half_l,
    so_send,
    st_send,
    so_recv,
    st_recv,
    co_send,
    cs_send,
    co_first,
    cs_first,
    co_second,
    cs_second,
    ag,
    lhs,
    terms,
    y_send,
    y_recv,
    loc_sem,
    q_ss,
    q_rs,
    qf_ss,
    qf_rs,
    x_ss,
    x_rs,
    c_ss,
    c_rs,
    s_ss,
    s_rs,
    z_ss,
    z_rs,
    ax_ss,
    ax_rs,
    ac_ss,
    ac_rs,
    y_ss,
    y_rs,
):
    f32, bf16 = jnp.float32, jnp.bfloat16
    wide = lax.axis_index("wide")
    y = lax.axis_index("kv")
    chip = wide // 2
    core = wide % 2
    zc = chip // 2
    xc = chip % 2
    sibling = (chip * 2 + 1 - core, y)

    def at_chip(c):
        return (c * 2 + core, y)

    local_copies = [pltpu.make_async_copy(pre_hbm, pre, loc_sem.at[0])]
    local_copies += [
        pltpu.make_async_copy(
            suf_hbm.at[s], suf.at[s, pl.ds(0, SUF_ROWS)], loc_sem.at[1 + s]
        ) for s in range(HELD)
    ]
    local_copies.append(pltpu.make_async_copy(w_hbm, w, loc_sem.at[1 + HELD]))
    for copy in local_copies:
        copy.start()

    barrier = pltpu.get_barrier_semaphore()
    for d in range(1, CHIPS):
        pl.semaphore_signal(
            barrier, inc=1, device_id=at_chip((chip + d) % CHIPS), device_id_type=MESH
        )
    pl.semaphore_signal(barrier, inc=1, device_id=sibling, device_id_type=MESH)
    pl.semaphore_signal(barrier, inc=1, device_id=(wide, 1 - y), device_id_type=MESH)

    prompts = [sprompt_ref[wide * HELD + s] for s in range(HELD)]
    groups = [pslot_ref[p] for p in prompts]
    ranks = []
    for s in range(HELD):
        rank = jnp.int32(0)
        for e in range(s):
            rank = rank + jnp.where(prompts[e] == prompts[s], 1, 0)
        ranks.append(rank)
    for c in range(CHIPS):
        for m in range(MOST):
            pick = jnp.int32(0)
            for s in range(1, HELD):
                pick = pick + jnp.where((groups[s] == c) & (ranks[s] == m), s, 0)
            chosen = q_ref[pick]
            for h in range(2):
                qslot[h, c, m * PART : (m + 1) * PART, :] = chosen[h * PART : (h + 1) * PART]
    prompt_rows = jnp.int32(0)
    for p in range(NPROMPT):
        prompt_rows = prompt_rows + jnp.where(pslot_ref[p] == chip, plen_ref[p], 0)

    out_row = lax.broadcasted_iota(jnp.int32, (256, 256), 0)
    in_row = lax.broadcasted_iota(jnp.int32, (256, 256), 1)
    split_p[...] = jnp.where(in_row == (out_row & 31) * 8 + (out_row >> 5), 1.0, 0.0).astype(bf16)
    gathered = ((out_row >> 1) & 3) * 64 + (out_row >> 3) * 2 + (out_row & 1)
    out_p[...] = jnp.where(in_row == gathered, 1.0, 0.0).astype(bf16)
    to_row, from_row = out_row[:128, :128], in_row[:128, :128]
    source = ((to_row >> 1) & 3) * PART + (to_row >> 3) * 2 + (to_row & 1)
    turn_p[...] = jnp.where(from_row == source, 1.0, 0.0).astype(bf16)

    pl.semaphore_wait(barrier, CHIPS + 1)

    q_copies = {}
    for h in range(2):
        for d in (4, 3, 5, 2, 6, 1, 7):
            dst = (chip + d) % CHIPS
            q_copies[h, d] = pltpu.make_async_remote_copy(
                src_ref=qslot.at[h, dst],
                dst_ref=qrecv.at[h, core, chip],
                send_sem=q_ss.at[8 * h + d],
                recv_sem=q_rs.at[8 * h + d],
                device_id=at_chip(dst),
                device_id_type=MESH,
            )
            q_copies[h, d].start()
        qrecv[h, core, chip] = qslot[h, chip]
    forwards = {}

    def forward(h, d):
        src = (chip + CHIPS - d) % CHIPS
        if d:
            q_copies[h, d].wait_recv()
        forwards[h, d] = pltpu.make_async_remote_copy(
            src_ref=qrecv.at[h, core, src],
            dst_ref=qrecv.at[h, core, src],
            send_sem=qf_ss.at[8 * h + d],
            recv_sem=qf_rs.at[8 * h + d],
            device_id=sibling,
            device_id_type=MESH,
        )
        forwards[h, d].start()

    forward(0, 0)
    forward(1, 0)

    local_copies[0].wait()
    for i in range(8):
        rows = jnp.concatenate(
            [pre[i * 512 : i * 512 + 256, :], pre[i * 512 + 256 : (i + 1) * 512, :]], axis=1
        )
        parted = jnp.dot(split_p[...], rows, preferred_element_type=f32).astype(bf16)
        for k in range(8):
            pkv[k, i * 64 : i * 64 + 32, :] = parted[k * 32 : (k + 1) * 32, :HD]
            pkv[k, i * 64 + 32 : (i + 1) * 64, :] = parted[k * 32 : (k + 1) * 32, HD:]

    col = lax.broadcasted_iota(jnp.int32, (SPAN, LOCAL), 1)
    row = lax.broadcasted_iota(jnp.int32, (SPAN, LOCAL), 0)
    spot = col >> 3
    fresh = jnp.where(spot - SUF <= (row & 1), -1, FAR)
    place[...] = jnp.where((col & 7) == (row >> 4), jnp.where(spot < SUF, spot, fresh), FAR)

    def local_part(s):
        local_copies[1 + s].wait()
        suf[s, SUF_ROWS : SUF_ROWS + 16, :] = new_ref[s]
        suf[s, SUF_ROWS + 16 :, :] = jnp.zeros((LOCAL - SUF_ROWS - 16, HD), bf16)
        scores = lax.dot_general(q_ref[s], suf[s], NT, preferred_element_type=f32)
        masked = jnp.where(place[...] < slen_ref[s], scores * SCALE2, -1e30)
        top = jnp.max(masked, axis=1, keepdims=True)
        weights = jnp.exp2(masked - top)
        total = jnp.sum(weights, axis=1, keepdims=True)
        moved = pltpu.roll(weights, KVL, 1).astype(bf16)
        lo[s] = jnp.dot(moved, suf[s], preferred_element_type=f32)
        lm[s] = jnp.broadcast_to(top, (SPAN, HD))
        ll[s] = jnp.broadcast_to(total, (SPAN, HD))

    local_part(0)
    for d in (1, 7, 2, 6, 3, 5, 4):
        forward(0, d)
    local_part(1)

    usable = lax.broadcasted_iota(jnp.int32, (256, PSH), 1) < prompt_rows - core * PSH

    def prefix_half(h, which):
        queries = qrecv[h, which].reshape(CHIPS, MOST, 2, ROWS, HD)
        for e in range(2):
            g = 2 * h + e
            query = queries[:, :, e].reshape(256, HD)
            scores = lax.dot_general(query, pkv[g], NT, preferred_element_type=f32)
            masked = jnp.where(usable, scores * SCALE2, -1e30)
            top = jnp.max(masked, axis=1, keepdims=True)
            weights = jnp.exp2(masked - top)
            total = jnp.sum(weights, axis=1, keepdims=True)
            result = jnp.dot(weights.astype(bf16), pkv[KVL + g], preferred_element_type=f32)
            shape = (CHIPS, MOST, ROWS, HD)
            half_o[:, :, e] = result.reshape(shape)
            half_m[:, :, e] = jnp.broadcast_to(top, (256, HD)).reshape(shape)
            half_l[:, :, e] = jnp.broadcast_to(total, (256, HD)).reshape(shape)

    def stat_rows(top, total):
        return jnp.concatenate([top, total], axis=0).T[:8]

    def flat(ref, c):
        return ref[c].reshape(PAIR, HD)

    co_recv, cs_recv = (co_first, co_second), (cs_first, cs_second)
    swaps = []
    results = {}

    def merge(h, c):
        m1, l1 = flat(half_m, c), flat(half_l, c)
        other = jnp.broadcast_to(st_recv[h, c][0:1], (HD, HD)).T
        m2, l2 = other[:PAIR], other[PAIR:]
        top = jnp.maximum(m1, m2)
        w1, w2 = jnp.exp2(m1 - top), jnp.exp2(m2 - top)
        total = w1 * l1 + w2 * l2
        mixed = w1 * flat(half_o, c) + w2 * so_recv[h, c].astype(f32)
        return (mixed / total).astype(bf16), stat_rows(top, total)

    def prefix_part(h):
        for d in range(CHIPS):
            forwards[h, d].wait_recv()
        prefix_half(h, 1 - core)
        for c in range(CHIPS):
            so_send[h, c] = flat(half_o, c).astype(bf16)
            st_send[h, c] = stat_rows(flat(half_m, c), flat(half_l, c))
        mine = []
        for i, (src, dst) in enumerate(((so_send, so_recv), (st_send, st_recv))):
            copy = pltpu.make_async_remote_copy(
                src_ref=src.at[h],
                dst_ref=dst.at[h],
                send_sem=x_ss.at[2 * h + i],
                recv_sem=x_rs.at[2 * h + i],
                device_id=sibling,
                device_id_type=MESH,
            )
            copy.start()
            mine.append(copy)
        swaps.extend(mine)
        prefix_half(h, core)
        for copy in mine:
            copy.wait_recv()
        for d in (4, 3, 5, 2, 6, 1, 7):
            dst = (chip + d) % CHIPS
            co_send[h, dst], cs_send[h, dst] = merge(h, dst)
            for src, target, ss, rs in (
                (co_send, co_recv, c_ss, c_rs),
                (cs_send, cs_recv, s_ss, s_rs),
            ):
                copy = pltpu.make_async_remote_copy(
                    src_ref=src.at[h, dst],
                    dst_ref=target[h].at[chip],
                    send_sem=ss.at[8 * h + d],
                    recv_sem=rs.at[8 * h + d],
                    device_id=at_chip(dst),
                    device_id_type=MESH,
                )
                copy.start()
                results.setdefault(h, []).append(copy)
        co_recv[h][chip], cs_recv[h][chip] = merge(h, chip)

    prefix_part(0)
    for d in (1, 7, 2, 6, 3, 5, 4):
        forward(1, d)
    local_part(2)
    prefix_part(1)
    local_part(3)

    def attention(h):
        for copy in results[h]:
            copy.wait_recv()
        here = slice(h * PART, (h + 1) * PART)
        parts = []
        for s in range(HELD):
            stats = jnp.broadcast_to(cs_recv[h][groups[s]][0:1], (HD, HD)).T
            block = co_recv[h][groups[s]].astype(f32)
            first = jnp.broadcast_to(ranks[s] == 0, (PART, HD))
            pm = jnp.where(first, stats[:PART], stats[PART:PAIR])
            pt = jnp.where(first, stats[PAIR : PAIR + PART], stats[PAIR + PART :])
            po = jnp.where(first, block[:PART], block[PART:])
            own = lm[s, here, :]
            overall = jnp.maximum(pm, own)
            wp = pt * jnp.exp2(pm - overall)
            wl = jnp.exp2(own - overall)
            mixed = wp * po + wl * lo[s, here, :]
            parts.append((mixed / (wp + wl * ll[s, here, :])).astype(bf16))
        attn = jnp.concatenate(parts, axis=0)
        turned = jnp.dot(turn_p[...], attn, preferred_element_type=f32)
        ag[h, wide] = turned.astype(bf16)

    sends = []

    def push(index, ss, rs, i, device):
        copy = pltpu.make_async_remote_copy(
            src_ref=ag.at[index],
            dst_ref=ag.at[index],
            send_sem=ss.at[i],
            recv_sem=rs.at[i],
            device_id=device,
            device_id_type=MESH,
        )
        copy.start()
        sends.append(copy)
        return copy

    x_peer = at_chip(zc * 2 + 1 - xc)
    z_in, x_in, c_in = {}, {}, ([], [])
    for h in range(2):
        attention(h)
        x_in[h, 0] = push((h, wide), ax_ss, ax_rs, 4 * h, x_peer)
        for d in (2, 1, 3):
            device = at_chip(((zc + d) % 4) * 2 + xc)
            z_in[h, d] = push((h, wide), z_ss, z_rs, 4 * h + d, device)
        c_in[h].append(push((h, wide), ac_ss, ac_rs, 8 * h, sibling))

    def pass_x(h, d):
        x_in[h, d].wait_recv()
        index = (((zc + 4 - d) % 4) * 2 + 1 - xc) * 2 + core
        c_in[h].append(push((h, index), ac_ss, ac_rs, 8 * h + 4 + d, sibling))

    def pass_z(h, d):
        z_in[h, d].wait_recv()
        index = (((zc + 4 - d) % 4) * 2 + xc) * 2 + core
        x_in[h, d] = push((h, index), ax_ss, ax_rs, 4 * h + d, x_peer)
        c_in[h].append(push((h, index), ac_ss, ac_rs, 8 * h + d, sibling))

    def gather_rows(h):
        for copy in c_in[h]:
            copy.wait_recv()
        for k in range(8):
            block = ag[h, :, k * 16 : (k + 1) * 16, :].astype(f32)
            to = h * 2048 + k * 256
            lhs[:, to : to + 128] = block[:, :8].reshape(128, HD).astype(bf16)
            lhs[:, to + 128 : to + 256] = block[:, 8:].reshape(128, HD).astype(bf16)

    for d in (1, 3, 2):
        pass_z(0, d)
    for d in (0, 1, 3, 2):
        pass_x(0, d)
    for d in (1, 3, 2):
        pass_z(1, d)
    local_copies[1 + HELD].wait()
    gather_rows(0)
    for n in range(2):
        terms[n] = jnp.dot(
            lhs[:, :2048], w[:2048, n * 256 : (n + 1) * 256], preferred_element_type=f32
        )
    for d in (0, 1, 3, 2):
        pass_x(1, d)
    gather_rows(1)

    theirs = pl.multiple_of((1 - y) * 64, 64)
    mine = pl.multiple_of(y * 64, 64)
    y_copies = []
    for n in range(2):
        terms[n] += jnp.dot(
            lhs[:, 2048:], w[2048:, n * 256 : (n + 1) * 256], preferred_element_type=f32
        )
        y_send[n] = terms[n, pl.ds(theirs, 64), :].astype(bf16)
        copy = pltpu.make_async_remote_copy(
            src_ref=y_send.at[n],
            dst_ref=y_recv.at[n],
            send_sem=y_ss.at[n],
            recv_sem=y_rs.at[n],
            device_id=(wide, 1 - y),
            device_id_type=MESH,
        )
        copy.start()
        y_copies.append(copy)
    finals = []
    for n in range(2):
        y_copies[n].wait_recv()
        total = terms[n, pl.ds(mine, 64), :] + y_recv[n].astype(f32)
        finals += [total[:, :HD].astype(bf16), total[:, HD:].astype(bf16)]
    o_ref[...] = jnp.dot(
        out_p[...], jnp.concatenate(finals, axis=0), preferred_element_type=f32
    ).astype(bf16)

    for copy in [*sends, *y_copies, *q_copies.values(), *forwards.values(), *swaps, *results[0], *results[1]]:
        copy.wait_send()


def fused_device(
    queries,
    new_kv,
    suffix_cache,
    suffix_len,
    prefix_cache,
    prompt_len,
    prompt_slot,
    sample_prompt,
    out_weight,
):
    f32, bf16 = jnp.float32, jnp.bfloat16
    q_rows = queries.reshape(HELD, STEPS, KVL * GROUP, HD).transpose(0, 2, 1, 3)
    q_rows = q_rows.reshape(HELD, SPAN, HD)
    new_rows = new_kv.reshape(HELD, STEPS, KVL, 2, HD).transpose(0, 1, 3, 2, 4)
    new_rows = new_rows.reshape(HELD, STEPS * 8, HD)
    suf = suffix_cache.reshape(HELD, SUF, KVL, 2, HD).transpose(0, 1, 3, 2, 4)
    suf = suf.reshape(HELD, SUF * 8, HD)
    pre = prefix_cache.reshape(PSH, KVL, 2, HD).transpose(0, 2, 1, 3).reshape(PSH * 8, HD)
    vm, sm, hbm = pltpu.VMEM, pltpu.SMEM, pl.ANY
    dma = pltpu.SemaphoreType.DMA
    half = (CHIPS, MOST, 2, ROWS, HD)
    block, stat = vm((2, CHIPS, PAIR, HD), bf16), vm((2, CHIPS, 8, HD), f32)
    scratch = [
        vm((HELD, LOCAL, HD), bf16),
        vm((PSH * 8, HD), bf16),
        vm((KVL * 1024, 512), bf16),
        vm((256, 256), bf16),
        vm((128, 128), bf16),
        vm((256, 256), bf16),
        vm((SPAN, LOCAL), jnp.int32),
        vm((8, PSH, HD), bf16),
        block,
        vm((2, 2, CHIPS, PAIR, HD), bf16),
        vm((HELD, SPAN, HD), f32),
        vm((HELD, SPAN, HD), f32),
        vm((HELD, SPAN, HD), f32),
        vm(half, f32),
        vm(half, f32),
        vm(half, f32),
        block,
        stat,
        block,
        stat,
        block,
        stat,
        vm((CHIPS, PAIR, HD), bf16),
        vm((CHIPS, 8, HD), f32),
        vm((CHIPS, PAIR, HD), bf16),
        vm((CHIPS, 8, HD), f32),
        vm((2, 16, 128, HD), bf16),
        vm((128, 4096), bf16),
        vm((2, 128, 256), f32),
        vm((2, 64, 256), bf16),
        vm((2, 64, 256), bf16),
        dma((2 + HELD,)),
    ]
    for count in (16, 16, 4, 16, 16, 8, 8, 16, 2):
        scratch += [dma((count,)), dma((count,))]
    out = pl.pallas_call(
        fused_kernel,
        out_shape=jax.ShapeDtypeStruct((256, HD), bf16),
        in_specs=[pl.BlockSpec(memory_space=sm)] * 4
        + [pl.BlockSpec(memory_space=vm)] * 2
        + [pl.BlockSpec(memory_space=hbm)] * 3,
        out_specs=pl.BlockSpec(memory_space=vm),
        scratch_shapes=scratch,
        compiler_params=pltpu.CompilerParams(
            collective_id=0, has_side_effects=True, vmem_limit_bytes=56 * 1024 * 1024
        ),
        cost_estimate=pl.CostEstimate(
            flops=4_000_000_000, bytes_accessed=12_000_000, transcendentals=1_500_000
        ),
    )(
        suffix_len,
        prompt_len,
        prompt_slot,
        sample_prompt.reshape(-1),
        q_rows,
        new_rows,
        suf,
        pre,
        out_weight,
    )
    return out.reshape(32, 4, STEPS, HD).transpose(0, 2, 1, 3).reshape(32, STEPS, 512)


def solution(mesh):
    small = mesh.shape["wide"] == 2 * CHIPS and mesh.shape["kv"] == 2
    return jax.shard_map(
        fused_device if small else general_device,
        mesh=mesh,
        in_specs=(
            P("wide", None, "kv"),
            P("wide", None, "kv", None),
            P("wide", None, "kv", None),
            P("wide"),
            P("wide", "kv", None),
            P(),
            P(),
            P(),
            P("kv", "wide"),
        ),
        out_specs=P("kv", None, "wide"),
        check_vma=False,
    )
```

```python
import functools
import math

import jax
import jax.numpy as jnp
from jax import lax
from jax.experimental import pallas as pl
from jax.experimental.pallas import tpu as pltpu
from jax.sharding import PartitionSpec as P

HD = 128
GROUP = 8
STEPS = 2
PSH = 512
SUF = 512
NPROMPT = 8
MOST = 2


def sample_ranks(prompt_block):
    length = prompt_block.shape[-1]
    earlier = jnp.arange(length)[None, :] < jnp.arange(length)[:, None]
    matching = prompt_block[..., :, None] == prompt_block[..., None, :]
    return jnp.sum(matching & earlier, axis=-1)


def prefix_part(slots, prefix_cache, prompt_rows, segment):
    sources = slots.shape[0]
    item_count = slots.shape[1]
    kv_local = prefix_cache.shape[1]
    batch_rows = sources * item_count * STEPS
    scale = HD ** (-0.5)
    key_rows = prefix_cache[:, :, :HD]
    value_rows = prefix_cache[:, :, HD:]
    usable = segment * PSH + jnp.arange(PSH) < prompt_rows
    block_rows = math.gcd(batch_rows, max(1, 512 // (kv_local * GROUP)))

    def one_block(query_block):
        scores = (
            jnp.einsum("bgxd,jgd->bgxj", query_block, key_rows, preferred_element_type=jnp.float32)
            * scale
        )
        masked = jnp.where(usable, scores, -1e30)
        row_max = jnp.max(masked, axis=-1)
        weights = jnp.where(usable, jnp.exp(masked - row_max[..., None]), 0.0)
        row_sum = jnp.sum(weights, axis=-1)
        weights_bf = (weights / jnp.maximum(row_sum, 1.0)[..., None]).astype(jnp.bfloat16)
        result = jnp.einsum(
            "bgxj,jgd->bgxd", weights_bf, value_rows, preferred_element_type=jnp.float32
        )
        return (result.astype(jnp.bfloat16), row_max, row_sum)

    query_blocks = slots.reshape(batch_rows // block_rows, block_rows, kv_local, GROUP, HD)
    results = lax.map(one_block, query_blocks)
    part_out = results[0].reshape(sources, item_count, -1)
    part_max = results[1].reshape(sources, item_count, -1)
    part_sum = results[2].reshape(sources, item_count, -1)
    part_out = lax.all_to_all(part_out, "wide", split_axis=0, concat_axis=0, tiled=True)
    part_max, part_sum = (
        lax.all_to_all(part_max, "wide", split_axis=0, concat_axis=0, tiled=True),
        lax.all_to_all(part_sum, "wide", split_axis=0, concat_axis=0, tiled=True),
    )
    return (part_out, part_max, part_sum)


def general_device(
    queries,
    new_kv,
    suffix_cache,
    suffix_len,
    prefix_cache,
    prompt_len,
    prompt_slot,
    sample_prompt,
    out_weight,
):
    wide_count = lax.axis_size("wide")
    split_count = wide_count // NPROMPT
    position = lax.axis_index("wide")
    held_rows = queries.shape[0]
    kv_local = new_kv.shape[2]
    scale = HD ** (-0.5)
    prompt_ids = sample_prompt[:, 0]
    my_prompts = lax.dynamic_slice_in_dim(prompt_ids, position * held_rows, held_rows)
    prompt_range = jnp.arange(NPROMPT)
    slot_range = jnp.arange(MOST)
    my_group = jnp.sum(
        jnp.where(my_prompts[:, None] == prompt_range[None, :], prompt_slot[None, :], 0), axis=1
    )
    my_rank = sample_ranks(my_prompts)
    picked = (my_group[:, None, None] == prompt_range[None, :, None]) & (
        my_rank[:, None, None] == slot_range[None, None, :]
    )
    own_group = position // split_count
    segment = position % split_count
    owner_match = prompt_slot == own_group
    prompt_rows = jnp.sum(jnp.where(owner_match, prompt_len, 0))
    own_prompt = jnp.sum(jnp.where(owner_match, prompt_range, 0))
    flat_queries = queries.reshape(held_rows, -1)
    everyone = lax.all_gather(flat_queries, "wide", axis=0, tiled=True)
    blocks = prompt_ids.reshape(wide_count, held_rows)
    block_rank = sample_ranks(blocks)
    chosen = (blocks[:, :, None] == own_prompt) & (
        block_rank[:, :, None] == slot_range[None, None, :]
    )
    incoming = jnp.einsum(
        "hrc,hrx->hcx",
        chosen.astype(jnp.bfloat16),
        everyone.reshape(wide_count, held_rows, -1),
        preferred_element_type=jnp.float32,
    ).astype(jnp.bfloat16)
    part_out, part_max, part_sum = prefix_part(incoming, prefix_cache, prompt_rows, segment)
    picked_bf = picked.astype(jnp.bfloat16)
    picked_f32 = picked.astype(jnp.float32)
    prefix_out = jnp.einsum(
        "rgc,gscx->rsx",
        picked_bf,
        part_out.reshape(NPROMPT, split_count, MOST, -1),
        preferred_element_type=jnp.float32,
    )
    prefix_max = jnp.einsum(
        "rgc,gscy->rsy",
        picked_f32,
        part_max.reshape(NPROMPT, split_count, MOST, -1),
        precision=lax.Precision.HIGHEST,
    )
    prefix_sum = jnp.einsum(
        "rgc,gscy->rsy",
        picked_f32,
        part_sum.reshape(NPROMPT, split_count, MOST, -1),
        precision=lax.Precision.HIGHEST,
    )
    prefix_out = prefix_out.reshape(held_rows, split_count, STEPS, kv_local, GROUP, HD)
    prefix_max = prefix_max.reshape(held_rows, split_count, STEPS, kv_local, GROUP)
    prefix_sum = prefix_sum.reshape(held_rows, split_count, STEPS, kv_local, GROUP)
    query_rows = queries.reshape(held_rows, STEPS, kv_local, GROUP, HD)
    local_rows = jnp.concatenate([suffix_cache, new_kv], axis=1)
    local_scores = (
        jnp.einsum(
            "stgxd,sjgd->stgxj",
            query_rows,
            local_rows[..., :HD],
            preferred_element_type=jnp.float32,
        )
        * scale
    )
    positions = jnp.arange(SUF + STEPS)
    step_ids = jnp.arange(STEPS)
    local_ok = jnp.where(
        positions[None, None, :] < SUF,
        positions[None, None, :] < suffix_len[:, None, None],
        positions[None, None, :] - SUF <= step_ids[None, :, None],
    )
    local_ok = local_ok[:, :, None, None, :]
    local_masked = jnp.where(local_ok, local_scores, -1e30)
    local_max = jnp.max(local_masked, axis=-1)
    local_weights = jnp.where(local_ok, jnp.exp(local_masked - local_max[..., None]), 0.0)
    local_sum = jnp.sum(local_weights, axis=-1)
    local_bf = (local_weights / local_sum[..., None]).astype(jnp.bfloat16)
    local_out = jnp.einsum(
        "stgxj,sjgd->stgxd", local_bf, local_rows[..., HD:], preferred_element_type=jnp.float32
    )
    overall = jnp.maximum(jnp.max(prefix_max, axis=1), local_max)
    seg_weight = prefix_sum * jnp.exp(prefix_max - overall[:, None])
    local_weight = local_sum * jnp.exp(local_max - overall)
    numerator = (
        jnp.sum(seg_weight[..., None] * prefix_out, axis=1) + local_weight[..., None] * local_out
    )
    denominator = jnp.sum(seg_weight, axis=1) + local_weight
    attn = (numerator / denominator[..., None]).astype(jnp.bfloat16).reshape(held_rows, STEPS, -1)
    terms = jnp.einsum(
        "stk,kd->std",
        lax.all_gather(attn, "wide", axis=0, tiled=True),
        out_weight,
        preferred_element_type=jnp.float32,
    )
    summed = lax.psum_scatter(terms, "kv", scatter_dimension=0, tiled=True)
    return summed.astype(jnp.bfloat16)


MESH = pl.DeviceIdType.MESH
CHIPS = 8
HELD = 4
KVL = 4
ROWS = STEPS * GROUP
SPAN = KVL * ROWS
PART = SPAN // 2
PAIR = MOST * PART
SUF_ROWS = SUF * 2 * KVL
LOCAL = SUF_ROWS + 256
WING = LOCAL // 2
FAR = 1 << 20
SCALE2 = HD ** (-0.5) * math.log2(math.e)
NT = (((1,), (1,)), ((), ()))


def fused_kernel(
    slen_ref,
    plen_ref,
    pslot_ref,
    sprompt_ref,
    q_ref,
    new_ref,
    suf_hbm,
    pre_hbm,
    w_hbm,
    o_ref,
    suf,
    pre,
    w,
    split_p,
    turn_p,
    out_p,
    place,
    pkv,
    qslot,
    qrecv,
    lo,
    lm,
    ll,
    half_o,
    half_m,
    half_l,
    so_send,
    st_send,
    so_recv,
    st_recv,
    co_send,
    cs_send,
    co_first,
    cs_first,
    co_second,
    cs_second,
    ag,
    lhs,
    terms,
    y_send,
    y_recv,
    loc_sem,
    q_ss,
    q_rs,
    qf_ss,
    qf_rs,
    x_ss,
    x_rs,
    c_ss,
    c_rs,
    s_ss,
    s_rs,
    z_ss,
    z_rs,
    ax_ss,
    ax_rs,
    ac_ss,
    ac_rs,
    y_ss,
    y_rs,
):
    f32, bf16 = jnp.float32, jnp.bfloat16
    wide = lax.axis_index("wide")
    y = lax.axis_index("kv")
    chip = wide // 2
    core = wide % 2
    zc = chip // 2
    xc = chip % 2
    sibling = (chip * 2 + 1 - core, y)

    def at_chip(c):
        return (c * 2 + core, y)

    local_copies = [pltpu.make_async_copy(pre_hbm, pre, loc_sem.at[0])]
    local_copies += [
        pltpu.make_async_copy(
            suf_hbm.at[s], suf.at[s, pl.ds(0, SUF_ROWS)], loc_sem.at[1 + s]
        ) for s in range(HELD)
    ]
    local_copies.append(pltpu.make_async_copy(w_hbm, w, loc_sem.at[1 + HELD]))
    for copy in local_copies:
        copy.start()

    barrier = pltpu.get_barrier_semaphore()
    for d in range(1, CHIPS):
        pl.semaphore_signal(
            barrier, inc=1, device_id=at_chip((chip + d) % CHIPS), device_id_type=MESH
        )
    pl.semaphore_signal(barrier, inc=1, device_id=sibling, device_id_type=MESH)
    pl.semaphore_signal(barrier, inc=1, device_id=(wide, 1 - y), device_id_type=MESH)

    prompts = [sprompt_ref[wide * HELD + s] for s in range(HELD)]
    groups = [pslot_ref[p] for p in prompts]
    ranks = []
    for s in range(HELD):
        rank = jnp.int32(0)
        for e in range(s):
            rank = rank + jnp.where(prompts[e] == prompts[s], 1, 0)
        ranks.append(rank)
    for c in range(CHIPS):
        for m in range(MOST):
            pick = jnp.int32(0)
            for s in range(1, HELD):
                pick = pick + jnp.where((groups[s] == c) & (ranks[s] == m), s, 0)
            chosen = q_ref[pick]
            for h in range(2):
                qslot[h, c, m * PART : (m + 1) * PART, :] = chosen[h * PART : (h + 1) * PART]
    prompt_rows = jnp.int32(0)
    for p in range(NPROMPT):
        prompt_rows = prompt_rows + jnp.where(pslot_ref[p] == chip, plen_ref[p], 0)

    pl.semaphore_wait(barrier, CHIPS + 1)

    q_copies = {}
    for h in range(2):
        for d in (4, 3, 5, 2, 6, 1, 7):
            dst = (chip + d) % CHIPS
            q_copies[h, d] = pltpu.make_async_remote_copy(
                src_ref=qslot.at[h, dst],
                dst_ref=qrecv.at[h, core, chip],
                send_sem=q_ss.at[8 * h + d],
                recv_sem=q_rs.at[8 * h + d],
                device_id=at_chip(dst),
                device_id_type=MESH,
            )
            q_copies[h, d].start()
        qrecv[h, core, chip] = qslot[h, chip]
    forwards = {}

    def forward(h, d):
        src = (chip + CHIPS - d) % CHIPS
        if d:
            q_copies[h, d].wait_recv()
        forwards[h, d] = pltpu.make_async_remote_copy(
            src_ref=qrecv.at[h, core, src],
            dst_ref=qrecv.at[h, core, src],
            send_sem=qf_ss.at[8 * h + d],
            recv_sem=qf_rs.at[8 * h + d],
            device_id=sibling,
            device_id_type=MESH,
        )
        forwards[h, d].start()

    forward(0, 0)
    forward(1, 0)

    out_row = lax.broadcasted_iota(jnp.int32, (256, 256), 0)
    in_row = lax.broadcasted_iota(jnp.int32, (256, 256), 1)
    split_p[...] = jnp.where(in_row == (out_row & 31) * 8 + (out_row >> 5), 1.0, 0.0).astype(bf16)
    gathered = ((out_row >> 1) & 3) * 64 + (out_row >> 3) * 2 + (out_row & 1)
    out_p[...] = jnp.where(in_row == gathered, 1.0, 0.0).astype(bf16)
    to_row, from_row = out_row[:128, :128], in_row[:128, :128]
    source = ((to_row >> 1) & 3) * PART + (to_row >> 3) * 2 + (to_row & 1)
    turn_p[...] = jnp.where(from_row == source, 1.0, 0.0).astype(bf16)

    local_copies[0].wait()
    for i in range(8):
        rows = jnp.concatenate(
            [pre[i * 512 : i * 512 + 256, :], pre[i * 512 + 256 : (i + 1) * 512, :]], axis=1
        )
        parted = jnp.dot(split_p[...], rows, preferred_element_type=f32).astype(bf16)
        for k in range(8):
            pkv[k, i * 64 : i * 64 + 32, :] = parted[k * 32 : (k + 1) * 32, :HD]
            pkv[k, i * 64 + 32 : (i + 1) * 64, :] = parted[k * 32 : (k + 1) * 32, HD:]

    col = lax.broadcasted_iota(jnp.int32, (2 * SPAN, WING), 1)
    row = lax.broadcasted_iota(jnp.int32, (2 * SPAN, WING), 0)
    spot = (col + jnp.where(row < SPAN, 0, WING)) >> 3
    fresh = jnp.where(spot - SUF <= (row & 1), -1, FAR)
    head = (row >> 4) & (KVL - 1)
    place[...] = jnp.where((col & 7) == head, jnp.where(spot < SUF, spot, fresh), FAR)
    blank = jnp.zeros((SPAN, HD), bf16)

    def local_part(s):
        local_copies[1 + s].wait()
        suf[s, SUF_ROWS : SUF_ROWS + 16, :] = new_ref[s]
        suf[s, SUF_ROWS + 16 :, :] = jnp.zeros((LOCAL - SUF_ROWS - 16, HD), bf16)
        wings = jnp.concatenate([suf[s, :WING, :], suf[s, WING:, :]], axis=1)
        query = jnp.concatenate(
            [
                jnp.concatenate([q_ref[s], blank], axis=1),
                jnp.concatenate([blank, q_ref[s]], axis=1),
            ],
            axis=0,
        )
        scores = lax.dot_general(query, wings, NT, preferred_element_type=f32)
        masked = jnp.where(place[...] < slen_ref[s], scores * SCALE2, -1e30)
        top = jnp.max(masked, axis=1, keepdims=True)
        top = jnp.maximum(top[:SPAN], top[SPAN:])
        weights = jnp.exp2(masked - jnp.concatenate([top, top], axis=0))
        total = jnp.sum(weights, axis=1, keepdims=True)
        moved = pltpu.roll(weights, KVL, 1).astype(bf16)
        mixed = jnp.dot(moved, wings, preferred_element_type=f32)
        lo[s] = mixed[:SPAN, :HD] + mixed[SPAN:, HD:]
        lm[s] = jnp.broadcast_to(top, (SPAN, HD))
        ll[s] = jnp.broadcast_to(total[:SPAN] + total[SPAN:], (SPAN, HD))

    local_part(0)
    for d in (1, 7, 2, 6, 3, 5, 4):
        forward(0, d)
    local_part(1)

    usable = lax.broadcasted_iota(jnp.int32, (256, PSH), 1) < prompt_rows - core * PSH

    def prefix_half(h, which):
        queries = qrecv[h, which].reshape(CHIPS, MOST, 2, ROWS, HD)
        for e in range(2):
            g = 2 * h + e
            query = queries[:, :, e].reshape(256, HD)
            scores = lax.dot_general(query, pkv[g], NT, preferred_element_type=f32)
            masked = jnp.where(usable, scores * SCALE2, -1e30)
            top = jnp.max(masked, axis=1, keepdims=True)
            weights = jnp.exp2(masked - top)
            total = jnp.sum(weights, axis=1, keepdims=True)
            result = jnp.dot(weights.astype(bf16), pkv[KVL + g], preferred_element_type=f32)
            shape = (CHIPS, MOST, ROWS, HD)
            half_o[:, :, e] = result.reshape(shape)
            half_m[:, :, e] = jnp.broadcast_to(top, (256, HD)).reshape(shape)
            half_l[:, :, e] = jnp.broadcast_to(total, (256, HD)).reshape(shape)

    def stat_rows(top, total):
        return jnp.concatenate([top, total], axis=0).T[:8]

    def flat(ref, c):
        return ref[c].reshape(PAIR, HD)

    co_recv, cs_recv = (co_first, co_second), (cs_first, cs_second)
    swaps = []
    results = {}

    def merge(h, c):
        m1, l1 = flat(half_m, c), flat(half_l, c)
        other = jnp.broadcast_to(st_recv[h, c][0:1], (HD, HD)).T
        m2, l2 = other[:PAIR], other[PAIR:]
        top = jnp.maximum(m1, m2)
        w1, w2 = jnp.exp2(m1 - top), jnp.exp2(m2 - top)
        total = w1 * l1 + w2 * l2
        mixed = w1 * flat(half_o, c) + w2 * so_recv[h, c].astype(f32)
        return (mixed / total).astype(bf16), stat_rows(top, total)

    def prefix_part(h):
        for d in range(CHIPS):
            forwards[h, d].wait_recv()
        prefix_half(h, 1 - core)
        for c in range(CHIPS):
            so_send[h, c] = flat(half_o, c).astype(bf16)
            st_send[h, c] = stat_rows(flat(half_m, c), flat(half_l, c))
        mine = []
        for i, (src, dst) in enumerate(((so_send, so_recv), (st_send, st_recv))):
            copy = pltpu.make_async_remote_copy(
                src_ref=src.at[h],
                dst_ref=dst.at[h],
                send_sem=x_ss.at[2 * h + i],
                recv_sem=x_rs.at[2 * h + i],
                device_id=sibling,
                device_id_type=MESH,
            )
            copy.start()
            mine.append(copy)
        swaps.extend(mine)
        prefix_half(h, core)
        for copy in mine:
            copy.wait_recv()
        for d in (4, 3, 5, 2, 6, 1, 7):
            dst = (chip + d) % CHIPS
            co_send[h, dst], cs_send[h, dst] = merge(h, dst)
            for src, target, ss, rs in (
                (co_send, co_recv, c_ss, c_rs),
                (cs_send, cs_recv, s_ss, s_rs),
            ):
                copy = pltpu.make_async_remote_copy(
                    src_ref=src.at[h, dst],
                    dst_ref=target[h].at[chip],
                    send_sem=ss.at[8 * h + d],
                    recv_sem=rs.at[8 * h + d],
                    device_id=at_chip(dst),
                    device_id_type=MESH,
                )
                copy.start()
                results.setdefault(h, []).append(copy)
        co_recv[h][chip], cs_recv[h][chip] = merge(h, chip)

    prefix_part(0)
    for d in (1, 7, 2, 6, 3, 5, 4):
        forward(1, d)
    prefix_part(1)
    local_part(2)
    local_part(3)

    def attention(h):
        for copy in results[h]:
            copy.wait_recv()
        here = slice(h * PART, (h + 1) * PART)
        parts = []
        for s in range(HELD):
            stats = jnp.broadcast_to(cs_recv[h][groups[s]][0:1], (HD, HD)).T
            block = co_recv[h][groups[s]].astype(f32)
            first = jnp.broadcast_to(ranks[s] == 0, (PART, HD))
            pm = jnp.where(first, stats[:PART], stats[PART:PAIR])
            pt = jnp.where(first, stats[PAIR : PAIR + PART], stats[PAIR + PART :])
            po = jnp.where(first, block[:PART], block[PART:])
            own = lm[s, here, :]
            overall = jnp.maximum(pm, own)
            wp = pt * jnp.exp2(pm - overall)
            wl = jnp.exp2(own - overall)
            mixed = wp * po + wl * lo[s, here, :]
            parts.append((mixed / (wp + wl * ll[s, here, :])).astype(bf16))
        attn = jnp.concatenate(parts, axis=0)
        turned = jnp.dot(turn_p[...], attn, preferred_element_type=f32)
        ag[h, wide] = turned.astype(bf16)

    sends = []

    def push(index, ss, rs, i, device):
        copy = pltpu.make_async_remote_copy(
            src_ref=ag.at[index],
            dst_ref=ag.at[index],
            send_sem=ss.at[i],
            recv_sem=rs.at[i],
            device_id=device,
            device_id_type=MESH,
        )
        copy.start()
        sends.append(copy)
        return copy

    x_peer = at_chip(zc * 2 + 1 - xc)
    z_in, x_in, c_in = {}, {}, ([], [])
    for h in range(2):
        attention(h)
        x_in[h, 0] = push((h, wide), ax_ss, ax_rs, 4 * h, x_peer)
        for d in (2, 1, 3):
            device = at_chip(((zc + d) % 4) * 2 + xc)
            z_in[h, d] = push((h, wide), z_ss, z_rs, 4 * h + d, device)
        c_in[h].append(push((h, wide), ac_ss, ac_rs, 8 * h, sibling))

    def pass_x(h, d):
        x_in[h, d].wait_recv()
        index = (((zc + 4 - d) % 4) * 2 + 1 - xc) * 2 + core
        c_in[h].append(push((h, index), ac_ss, ac_rs, 8 * h + 4 + d, sibling))

    def pass_z(h, d):
        z_in[h, d].wait_recv()
        index = (((zc + 4 - d) % 4) * 2 + xc) * 2 + core
        x_in[h, d] = push((h, index), ax_ss, ax_rs, 4 * h + d, x_peer)
        c_in[h].append(push((h, index), ac_ss, ac_rs, 8 * h + d, sibling))

    def gather_rows(h):
        for copy in c_in[h]:
            copy.wait_recv()
        for k in range(8):
            block = ag[h, :, k * 16 : (k + 1) * 16, :].astype(f32)
            to = h * 2048 + k * 256
            lhs[:, to : to + 128] = block[:, :8].reshape(128, HD).astype(bf16)
            lhs[:, to + 128 : to + 256] = block[:, 8:].reshape(128, HD).astype(bf16)

    for d in (1, 3, 2):
        pass_z(0, d)
    for d in (0, 1, 3, 2):
        pass_x(0, d)
    for d in (1, 3, 2):
        pass_z(1, d)
    local_copies[1 + HELD].wait()
    gather_rows(0)
    for n in range(2):
        terms[n] = jnp.dot(
            lhs[:, :2048], w[:2048, n * 256 : (n + 1) * 256], preferred_element_type=f32
        )
    for d in (0, 1, 3, 2):
        pass_x(1, d)
    gather_rows(1)

    theirs = pl.multiple_of((1 - y) * 64, 64)
    mine = pl.multiple_of(y * 64, 64)
    y_copies = []
    for n in range(2):
        terms[n] += jnp.dot(
            lhs[:, 2048:], w[2048:, n * 256 : (n + 1) * 256], preferred_element_type=f32
        )
        y_send[n] = terms[n, pl.ds(theirs, 64), :].astype(bf16)
        copy = pltpu.make_async_remote_copy(
            src_ref=y_send.at[n],
            dst_ref=y_recv.at[n],
            send_sem=y_ss.at[n],
            recv_sem=y_rs.at[n],
            device_id=(wide, 1 - y),
            device_id_type=MESH,
        )
        copy.start()
        y_copies.append(copy)
    finals = []
    for n in range(2):
        y_copies[n].wait_recv()
        total = terms[n, pl.ds(mine, 64), :] + y_recv[n].astype(f32)
        finals += [total[:, :HD].astype(bf16), total[:, HD:].astype(bf16)]
    o_ref[...] = jnp.dot(
        out_p[...], jnp.concatenate(finals, axis=0), preferred_element_type=f32
    ).astype(bf16)

    for copy in [*sends, *y_copies, *q_copies.values(), *forwards.values(), *swaps, *results[0], *results[1]]:
        copy.wait_send()


def fused_device(
    queries,
    new_kv,
    suffix_cache,
    suffix_len,
    prefix_cache,
    prompt_len,
    prompt_slot,
    sample_prompt,
    out_weight,
):
    f32, bf16 = jnp.float32, jnp.bfloat16
    q_rows = queries.reshape(HELD, STEPS, KVL * GROUP, HD).transpose(0, 2, 1, 3)
    q_rows = q_rows.reshape(HELD, SPAN, HD)
    new_rows = new_kv.reshape(HELD, STEPS, KVL, 2, HD).transpose(0, 1, 3, 2, 4)
    new_rows = new_rows.reshape(HELD, STEPS * 8, HD)
    suf = suffix_cache.reshape(HELD, SUF, KVL, 2, HD).transpose(0, 1, 3, 2, 4)
    suf = suf.reshape(HELD, SUF * 8, HD)
    pre = prefix_cache.reshape(PSH, KVL, 2, HD).transpose(0, 2, 1, 3).reshape(PSH * 8, HD)
    vm, sm, hbm = pltpu.VMEM, pltpu.SMEM, pl.ANY
    dma = pltpu.SemaphoreType.DMA
    half = (CHIPS, MOST, 2, ROWS, HD)
    block, stat = vm((2, CHIPS, PAIR, HD), bf16), vm((2, CHIPS, 8, HD), f32)
    scratch = [
        vm((HELD, LOCAL, HD), bf16),
        vm((PSH * 8, HD), bf16),
        vm((KVL * 1024, 512), bf16),
        vm((256, 256), bf16),
        vm((128, 128), bf16),
        vm((256, 256), bf16),
        vm((2 * SPAN, WING), jnp.int32),
        vm((8, PSH, HD), bf16),
        block,
        vm((2, 2, CHIPS, PAIR, HD), bf16),
        vm((HELD, SPAN, HD), f32),
        vm((HELD, SPAN, HD), f32),
        vm((HELD, SPAN, HD), f32),
        vm(half, f32),
        vm(half, f32),
        vm(half, f32),
        block,
        stat,
        block,
        stat,
        block,
        stat,
        vm((CHIPS, PAIR, HD), bf16),
        vm((CHIPS, 8, HD), f32),
        vm((CHIPS, PAIR, HD), bf16),
        vm((CHIPS, 8, HD), f32),
        vm((2, 16, 128, HD), bf16),
        vm((128, 4096), bf16),
        vm((2, 128, 256), f32),
        vm((2, 64, 256), bf16),
        vm((2, 64, 256), bf16),
        dma((2 + HELD,)),
    ]
    for count in (16, 16, 4, 16, 16, 8, 8, 16, 2):
        scratch += [dma((count,)), dma((count,))]
    out = pl.pallas_call(
        fused_kernel,
        out_shape=jax.ShapeDtypeStruct((256, HD), bf16),
        in_specs=[pl.BlockSpec(memory_space=sm)] * 4
        + [pl.BlockSpec(memory_space=vm)] * 2
        + [pl.BlockSpec(memory_space=hbm)] * 3,
        out_specs=pl.BlockSpec(memory_space=vm),
        scratch_shapes=scratch,
        compiler_params=pltpu.CompilerParams(
            collective_id=0, has_side_effects=True, vmem_limit_bytes=56 * 1024 * 1024
        ),
        cost_estimate=pl.CostEstimate(
            flops=4_000_000_000, bytes_accessed=12_000_000, transcendentals=1_500_000
        ),
    )(
        suffix_len,
        prompt_len,
        prompt_slot,
        sample_prompt.reshape(-1),
        q_rows,
        new_rows,
        suf,
        pre,
        out_weight,
    )
    return out.reshape(32, 4, STEPS, HD).transpose(0, 2, 1, 3).reshape(32, STEPS, 512)


def solution(mesh):
    small = mesh.shape["wide"] == 2 * CHIPS and mesh.shape["kv"] == 2
    return jax.shard_map(
        fused_device if small else general_device,
        mesh=mesh,
        in_specs=(
            P("wide", None, "kv"),
            P("wide", None, "kv", None),
            P("wide", None, "kv", None),
            P("wide"),
            P("wide", "kv", None),
            P(),
            P(),
            P(),
            P("kv", "wide"),
        ),
        out_specs=P("kv", None, "wide"),
        check_vma=False,
    )
```

```python
import functools
import math

import jax
import jax.numpy as jnp
from jax import lax
from jax.experimental import pallas as pl
from jax.experimental.pallas import tpu as pltpu
from jax.sharding import PartitionSpec as P

HD = 128
GROUP = 8
STEPS = 2
PSH = 512
SUF = 512
NPROMPT = 8
MOST = 2


def sample_ranks(prompt_block):
    length = prompt_block.shape[-1]
    earlier = jnp.arange(length)[None, :] < jnp.arange(length)[:, None]
    matching = prompt_block[..., :, None] == prompt_block[..., None, :]
    return jnp.sum(matching & earlier, axis=-1)


def prefix_part(slots, prefix_cache, prompt_rows, segment):
    sources = slots.shape[0]
    item_count = slots.shape[1]
    kv_local = prefix_cache.shape[1]
    batch_rows = sources * item_count * STEPS
    scale = HD ** (-0.5)
    key_rows = prefix_cache[:, :, :HD]
    value_rows = prefix_cache[:, :, HD:]
    usable = segment * PSH + jnp.arange(PSH) < prompt_rows
    block_rows = math.gcd(batch_rows, max(1, 512 // (kv_local * GROUP)))

    def one_block(query_block):
        scores = (
            jnp.einsum("bgxd,jgd->bgxj", query_block, key_rows, preferred_element_type=jnp.float32)
            * scale
        )
        masked = jnp.where(usable, scores, -1e30)
        row_max = jnp.max(masked, axis=-1)
        weights = jnp.where(usable, jnp.exp(masked - row_max[..., None]), 0.0)
        row_sum = jnp.sum(weights, axis=-1)
        weights_bf = (weights / jnp.maximum(row_sum, 1.0)[..., None]).astype(jnp.bfloat16)
        result = jnp.einsum(
            "bgxj,jgd->bgxd", weights_bf, value_rows, preferred_element_type=jnp.float32
        )
        return (result.astype(jnp.bfloat16), row_max, row_sum)

    query_blocks = slots.reshape(batch_rows // block_rows, block_rows, kv_local, GROUP, HD)
    results = lax.map(one_block, query_blocks)
    part_out = results[0].reshape(sources, item_count, -1)
    part_max = results[1].reshape(sources, item_count, -1)
    part_sum = results[2].reshape(sources, item_count, -1)
    part_out = lax.all_to_all(part_out, "wide", split_axis=0, concat_axis=0, tiled=True)
    part_max, part_sum = (
        lax.all_to_all(part_max, "wide", split_axis=0, concat_axis=0, tiled=True),
        lax.all_to_all(part_sum, "wide", split_axis=0, concat_axis=0, tiled=True),
    )
    return (part_out, part_max, part_sum)


def general_device(
    queries,
    new_kv,
    suffix_cache,
    suffix_len,
    prefix_cache,
    prompt_len,
    prompt_slot,
    sample_prompt,
    out_weight,
):
    wide_count = lax.axis_size("wide")
    split_count = wide_count // NPROMPT
    position = lax.axis_index("wide")
    held_rows = queries.shape[0]
    kv_local = new_kv.shape[2]
    scale = HD ** (-0.5)
    prompt_ids = sample_prompt[:, 0]
    my_prompts = lax.dynamic_slice_in_dim(prompt_ids, position * held_rows, held_rows)
    prompt_range = jnp.arange(NPROMPT)
    slot_range = jnp.arange(MOST)
    my_group = jnp.sum(
        jnp.where(my_prompts[:, None] == prompt_range[None, :], prompt_slot[None, :], 0), axis=1
    )
    my_rank = sample_ranks(my_prompts)
    picked = (my_group[:, None, None] == prompt_range[None, :, None]) & (
        my_rank[:, None, None] == slot_range[None, None, :]
    )
    own_group = position // split_count
    segment = position % split_count
    owner_match = prompt_slot == own_group
    prompt_rows = jnp.sum(jnp.where(owner_match, prompt_len, 0))
    own_prompt = jnp.sum(jnp.where(owner_match, prompt_range, 0))
    flat_queries = queries.reshape(held_rows, -1)
    everyone = lax.all_gather(flat_queries, "wide", axis=0, tiled=True)
    blocks = prompt_ids.reshape(wide_count, held_rows)
    block_rank = sample_ranks(blocks)
    chosen = (blocks[:, :, None] == own_prompt) & (
        block_rank[:, :, None] == slot_range[None, None, :]
    )
    incoming = jnp.einsum(
        "hrc,hrx->hcx",
        chosen.astype(jnp.bfloat16),
        everyone.reshape(wide_count, held_rows, -1),
        preferred_element_type=jnp.float32,
    ).astype(jnp.bfloat16)
    part_out, part_max, part_sum = prefix_part(incoming, prefix_cache, prompt_rows, segment)
    picked_bf = picked.astype(jnp.bfloat16)
    picked_f32 = picked.astype(jnp.float32)
    prefix_out = jnp.einsum(
        "rgc,gscx->rsx",
        picked_bf,
        part_out.reshape(NPROMPT, split_count, MOST, -1),
        preferred_element_type=jnp.float32,
    )
    prefix_max = jnp.einsum(
        "rgc,gscy->rsy",
        picked_f32,
        part_max.reshape(NPROMPT, split_count, MOST, -1),
        precision=lax.Precision.HIGHEST,
    )
    prefix_sum = jnp.einsum(
        "rgc,gscy->rsy",
        picked_f32,
        part_sum.reshape(NPROMPT, split_count, MOST, -1),
        precision=lax.Precision.HIGHEST,
    )
    prefix_out = prefix_out.reshape(held_rows, split_count, STEPS, kv_local, GROUP, HD)
    prefix_max = prefix_max.reshape(held_rows, split_count, STEPS, kv_local, GROUP)
    prefix_sum = prefix_sum.reshape(held_rows, split_count, STEPS, kv_local, GROUP)
    query_rows = queries.reshape(held_rows, STEPS, kv_local, GROUP, HD)
    local_rows = jnp.concatenate([suffix_cache, new_kv], axis=1)
    local_scores = (
        jnp.einsum(
            "stgxd,sjgd->stgxj",
            query_rows,
            local_rows[..., :HD],
            preferred_element_type=jnp.float32,
        )
        * scale
    )
    positions = jnp.arange(SUF + STEPS)
    step_ids = jnp.arange(STEPS)
    local_ok = jnp.where(
        positions[None, None, :] < SUF,
        positions[None, None, :] < suffix_len[:, None, None],
        positions[None, None, :] - SUF <= step_ids[None, :, None],
    )
    local_ok = local_ok[:, :, None, None, :]
    local_masked = jnp.where(local_ok, local_scores, -1e30)
    local_max = jnp.max(local_masked, axis=-1)
    local_weights = jnp.where(local_ok, jnp.exp(local_masked - local_max[..., None]), 0.0)
    local_sum = jnp.sum(local_weights, axis=-1)
    local_bf = (local_weights / local_sum[..., None]).astype(jnp.bfloat16)
    local_out = jnp.einsum(
        "stgxj,sjgd->stgxd", local_bf, local_rows[..., HD:], preferred_element_type=jnp.float32
    )
    overall = jnp.maximum(jnp.max(prefix_max, axis=1), local_max)
    seg_weight = prefix_sum * jnp.exp(prefix_max - overall[:, None])
    local_weight = local_sum * jnp.exp(local_max - overall)
    numerator = (
        jnp.sum(seg_weight[..., None] * prefix_out, axis=1) + local_weight[..., None] * local_out
    )
    denominator = jnp.sum(seg_weight, axis=1) + local_weight
    attn = (numerator / denominator[..., None]).astype(jnp.bfloat16).reshape(held_rows, STEPS, -1)
    terms = jnp.einsum(
        "stk,kd->std",
        lax.all_gather(attn, "wide", axis=0, tiled=True),
        out_weight,
        preferred_element_type=jnp.float32,
    )
    summed = lax.psum_scatter(terms, "kv", scatter_dimension=0, tiled=True)
    return summed.astype(jnp.bfloat16)


MESH = pl.DeviceIdType.MESH
CHIPS = 8
HELD = 4
KVL = 4
ROWS = STEPS * GROUP
SPAN = KVL * ROWS
PART = SPAN // 2
PAIR = MOST * PART
SUF_ROWS = SUF * 2 * KVL
LOCAL = SUF_ROWS + 256
WING = LOCAL // 2
FAR = 1 << 20
SCALE2 = HD ** (-0.5) * math.log2(math.e)
NT = (((1,), (1,)), ((), ()))


def fused_kernel(
    slen_ref,
    plen_ref,
    pslot_ref,
    sprompt_ref,
    q_ref,
    new_ref,
    suf_hbm,
    pre_hbm,
    w_hbm,
    o_ref,
    suf,
    pre,
    w,
    split_p,
    turn_p,
    out_p,
    place,
    pkv,
    qslot,
    qrecv,
    lo,
    lm,
    ll,
    half_o,
    half_m,
    half_l,
    so_send,
    st_send,
    so_recv,
    st_recv,
    co_send,
    cs_send,
    co_first,
    cs_first,
    co_second,
    cs_second,
    ag,
    lhs,
    terms,
    y_send,
    y_recv,
    loc_sem,
    q_ss,
    q_rs,
    qf_ss,
    qf_rs,
    x_ss,
    x_rs,
    c_ss,
    c_rs,
    s_ss,
    s_rs,
    z_ss,
    z_rs,
    ax_ss,
    ax_rs,
    ac_ss,
    ac_rs,
    y_ss,
    y_rs,
):
    f32, bf16 = jnp.float32, jnp.bfloat16
    wide = lax.axis_index("wide")
    y = lax.axis_index("kv")
    chip = wide // 2
    core = wide % 2
    zc = chip // 2
    xc = chip % 2
    sibling = (chip * 2 + 1 - core, y)

    def at_chip(c):
        return (c * 2 + core, y)

    local_copies = [pltpu.make_async_copy(pre_hbm, pre, loc_sem.at[0])]
    local_copies += [
        pltpu.make_async_copy(
            suf_hbm.at[s], suf.at[s, pl.ds(0, SUF_ROWS)], loc_sem.at[1 + s]
        ) for s in range(HELD)
    ]
    local_copies.append(pltpu.make_async_copy(w_hbm, w, loc_sem.at[1 + HELD]))
    for copy in local_copies:
        copy.start()

    barrier = pltpu.get_barrier_semaphore()
    for d in range(1, CHIPS):
        pl.semaphore_signal(
            barrier, inc=1, device_id=at_chip((chip + d) % CHIPS), device_id_type=MESH
        )
    pl.semaphore_signal(barrier, inc=1, device_id=sibling, device_id_type=MESH)
    pl.semaphore_signal(barrier, inc=1, device_id=(wide, 1 - y), device_id_type=MESH)

    prompts = [sprompt_ref[wide * HELD + s] for s in range(HELD)]
    groups = [pslot_ref[p] for p in prompts]
    ranks = []
    for s in range(HELD):
        rank = jnp.int32(0)
        for e in range(s):
            rank = rank + jnp.where(prompts[e] == prompts[s], 1, 0)
        ranks.append(rank)
    for c in range(CHIPS):
        for m in range(MOST):
            pick = jnp.int32(0)
            for s in range(1, HELD):
                pick = pick + jnp.where((groups[s] == c) & (ranks[s] == m), s, 0)
            chosen = q_ref[pick]
            for h in range(2):
                qslot[h, c, m * PART : (m + 1) * PART, :] = chosen[h * PART : (h + 1) * PART]
    prompt_rows = jnp.int32(0)
    for p in range(NPROMPT):
        prompt_rows = prompt_rows + jnp.where(pslot_ref[p] == chip, plen_ref[p], 0)

    pl.semaphore_wait(barrier, CHIPS + 1)

    q_copies = {}
    for h in range(2):
        for d in (4, 3, 5, 2, 6, 1, 7):
            dst = (chip + d) % CHIPS
            q_copies[h, d] = pltpu.make_async_remote_copy(
                src_ref=qslot.at[h, dst],
                dst_ref=qrecv.at[h, core, chip],
                send_sem=q_ss.at[8 * h + d],
                recv_sem=q_rs.at[8 * h + d],
                device_id=at_chip(dst),
                device_id_type=MESH,
            )
            q_copies[h, d].start()
        qrecv[h, core, chip] = qslot[h, chip]
    forwards = {}

    def forward(h, d):
        src = (chip + CHIPS - d) % CHIPS
        if d:
            q_copies[h, d].wait_recv()
        forwards[h, d] = pltpu.make_async_remote_copy(
            src_ref=qrecv.at[h, core, src],
            dst_ref=qrecv.at[h, core, src],
            send_sem=qf_ss.at[8 * h + d],
            recv_sem=qf_rs.at[8 * h + d],
            device_id=sibling,
            device_id_type=MESH,
        )
        forwards[h, d].start()

    forward(0, 0)
    forward(1, 0)

    out_row = lax.broadcasted_iota(jnp.int32, (256, 256), 0)
    in_row = lax.broadcasted_iota(jnp.int32, (256, 256), 1)
    split_p[...] = jnp.where(in_row == (out_row & 31) * 8 + (out_row >> 5), 1.0, 0.0).astype(bf16)
    gathered = ((out_row >> 1) & 3) * 64 + (out_row >> 3) * 2 + (out_row & 1)
    out_p[...] = jnp.where(in_row == gathered, 1.0, 0.0).astype(bf16)
    to_row, from_row = out_row[:128, :128], in_row[:128, :128]
    source = ((to_row >> 1) & 3) * PART + (to_row >> 3) * 2 + (to_row & 1)
    turn_p[...] = jnp.where(from_row == source, 1.0, 0.0).astype(bf16)

    local_copies[0].wait()
    for i in range(8):
        rows = jnp.concatenate(
            [pre[i * 512 : i * 512 + 256, :], pre[i * 512 + 256 : (i + 1) * 512, :]], axis=1
        )
        parted = jnp.dot(split_p[...], rows, preferred_element_type=f32).astype(bf16)
        for k in range(8):
            pkv[k, i * 64 : i * 64 + 32, :] = parted[k * 32 : (k + 1) * 32, :HD]
            pkv[k, i * 64 + 32 : (i + 1) * 64, :] = parted[k * 32 : (k + 1) * 32, HD:]

    col = lax.broadcasted_iota(jnp.int32, (2 * SPAN, WING), 1)
    row = lax.broadcasted_iota(jnp.int32, (2 * SPAN, WING), 0)
    spot = (col + jnp.where(row < SPAN, 0, WING)) >> 3
    fresh = jnp.where(spot - SUF <= (row & 1), -1, FAR)
    head = (row >> 4) & (KVL - 1)
    place[...] = jnp.where((col & 7) == head, jnp.where(spot < SUF, spot, fresh), FAR)
    blank = jnp.zeros((SPAN, HD), bf16)

    def local_part(s):
        local_copies[1 + s].wait()
        suf[s, SUF_ROWS : SUF_ROWS + 16, :] = new_ref[s]
        suf[s, SUF_ROWS + 16 :, :] = jnp.zeros((LOCAL - SUF_ROWS - 16, HD), bf16)
        wings = jnp.concatenate([suf[s, :WING, :], suf[s, WING:, :]], axis=1)
        query = jnp.concatenate(
            [
                jnp.concatenate([q_ref[s], blank], axis=1),
                jnp.concatenate([blank, q_ref[s]], axis=1),
            ],
            axis=0,
        )
        scores = lax.dot_general(query, wings, NT, preferred_element_type=f32)
        masked = jnp.where(place[...] < slen_ref[s], scores * SCALE2, -1e30)
        top = jnp.max(masked, axis=1, keepdims=True)
        top = jnp.maximum(top[:SPAN], top[SPAN:])
        weights = jnp.exp2(masked - jnp.concatenate([top, top], axis=0))
        total = jnp.sum(weights, axis=1, keepdims=True)
        moved = pltpu.roll(weights, KVL, 1).astype(bf16)
        mixed = jnp.dot(moved, wings, preferred_element_type=f32)
        lo[s] = mixed[:SPAN, :HD] + mixed[SPAN:, HD:]
        lm[s] = jnp.broadcast_to(top, (SPAN, HD))
        ll[s] = jnp.broadcast_to(total[:SPAN] + total[SPAN:], (SPAN, HD))

    local_part(0)
    for d in (1, 7, 2, 6, 3, 5, 4):
        forward(0, d)
    local_part(1)

    usable = lax.broadcasted_iota(jnp.int32, (256, PSH), 1) < prompt_rows - core * PSH

    def prefix_half(h, which):
        queries = qrecv[h, which].reshape(CHIPS, MOST, 2, ROWS, HD)
        for e in range(2):
            g = 2 * h + e
            query = queries[:, :, e].reshape(256, HD)
            scores = lax.dot_general(query, pkv[g], NT, preferred_element_type=f32)
            masked = jnp.where(usable, scores * SCALE2, -1e30)
            top = jnp.max(masked, axis=1, keepdims=True)
            weights = jnp.exp2(masked - top)
            total = jnp.sum(weights, axis=1, keepdims=True)
            result = jnp.dot(weights.astype(bf16), pkv[KVL + g], preferred_element_type=f32)
            shape = (CHIPS, MOST, ROWS, HD)
            half_o[:, :, e] = result.reshape(shape)
            half_m[:, :, e] = jnp.broadcast_to(top, (256, HD)).reshape(shape)
            half_l[:, :, e] = jnp.broadcast_to(total, (256, HD)).reshape(shape)

    def stat_rows(top, total):
        return jnp.concatenate([top, total], axis=0).T[:1]

    def flat(ref, c):
        return ref[c].reshape(PAIR, HD)

    co_recv, cs_recv = (co_first, co_second), (cs_first, cs_second)
    swaps = []
    results = {}

    def merge(h, c):
        m1, l1 = flat(half_m, c), flat(half_l, c)
        other = jnp.broadcast_to(st_recv[h, c][0:1], (HD, HD)).T
        m2, l2 = other[:PAIR], other[PAIR:]
        top = jnp.maximum(m1, m2)
        w1, w2 = jnp.exp2(m1 - top), jnp.exp2(m2 - top)
        total = w1 * l1 + w2 * l2
        mixed = w1 * flat(half_o, c) + w2 * so_recv[h, c].astype(f32)
        return (mixed / total).astype(bf16), stat_rows(top, total)

    def prefix_part(h):
        for d in range(CHIPS):
            forwards[h, d].wait_recv()
        prefix_half(h, 1 - core)
        for c in range(CHIPS):
            so_send[h, c] = flat(half_o, c).astype(bf16)
            st_send[h, c] = stat_rows(flat(half_m, c), flat(half_l, c))
        mine = []
        for i, (src, dst) in enumerate(((so_send, so_recv), (st_send, st_recv))):
            copy = pltpu.make_async_remote_copy(
                src_ref=src.at[h],
                dst_ref=dst.at[h],
                send_sem=x_ss.at[2 * h + i],
                recv_sem=x_rs.at[2 * h + i],
                device_id=sibling,
                device_id_type=MESH,
            )
            copy.start()
            mine.append(copy)
        swaps.extend(mine)
        prefix_half(h, core)
        if h == 0:
            for d in (1, 7, 2, 6, 3, 5, 4):
                forward(1, d)
        for copy in mine:
            copy.wait_recv()
        for d in (4, 3, 5, 2, 6, 1, 7):
            dst = (chip + d) % CHIPS
            co_send[h, dst], cs_send[h, dst] = merge(h, dst)
            for src, target, ss, rs in (
                (co_send, co_recv, c_ss, c_rs),
                (cs_send, cs_recv, s_ss, s_rs),
            ):
                copy = pltpu.make_async_remote_copy(
                    src_ref=src.at[h, dst],
                    dst_ref=target[h].at[chip],
                    send_sem=ss.at[8 * h + d],
                    recv_sem=rs.at[8 * h + d],
                    device_id=at_chip(dst),
                    device_id_type=MESH,
                )
                copy.start()
                results.setdefault(h, []).append(copy)
        co_recv[h][chip], cs_recv[h][chip] = merge(h, chip)

    prefix_part(0)
    prefix_part(1)
    local_part(2)
    local_part(3)

    def attention(h):
        for copy in results[h]:
            copy.wait_recv()
        here = slice(h * PART, (h + 1) * PART)
        parts = []
        for s in range(HELD):
            stats = jnp.broadcast_to(cs_recv[h][groups[s]][0:1], (HD, HD)).T
            block = co_recv[h][groups[s]].astype(f32)
            first = jnp.broadcast_to(ranks[s] == 0, (PART, HD))
            pm = jnp.where(first, stats[:PART], stats[PART:PAIR])
            pt = jnp.where(first, stats[PAIR : PAIR + PART], stats[PAIR + PART :])
            po = jnp.where(first, block[:PART], block[PART:])
            own = lm[s, here, :]
            overall = jnp.maximum(pm, own)
            wp = pt * jnp.exp2(pm - overall)
            wl = jnp.exp2(own - overall)
            mixed = wp * po + wl * lo[s, here, :]
            parts.append((mixed / (wp + wl * ll[s, here, :])).astype(bf16))
        attn = jnp.concatenate(parts, axis=0)
        turned = jnp.dot(turn_p[...], attn, preferred_element_type=f32)
        ag[h, wide] = turned.astype(bf16)

    sends = []

    def push(index, ss, rs, i, device):
        copy = pltpu.make_async_remote_copy(
            src_ref=ag.at[index],
            dst_ref=ag.at[index],
            send_sem=ss.at[i],
            recv_sem=rs.at[i],
            device_id=device,
            device_id_type=MESH,
        )
        copy.start()
        sends.append(copy)
        return copy

    x_peer = at_chip(zc * 2 + 1 - xc)
    z_in, x_in, c_in = {}, {}, ([], [])
    for h in range(2):
        attention(h)
        x_in[h, 0] = push((h, wide), ax_ss, ax_rs, 4 * h, x_peer)
        for d in (2, 1, 3):
            device = at_chip(((zc + d) % 4) * 2 + xc)
            z_in[h, d] = push((h, wide), z_ss, z_rs, 4 * h + d, device)
        c_in[h].append(push((h, wide), ac_ss, ac_rs, 8 * h, sibling))

    def pass_x(h, d):
        x_in[h, d].wait_recv()
        index = (((zc + 4 - d) % 4) * 2 + 1 - xc) * 2 + core
        c_in[h].append(push((h, index), ac_ss, ac_rs, 8 * h + 4 + d, sibling))

    def pass_z(h, d):
        z_in[h, d].wait_recv()
        index = (((zc + 4 - d) % 4) * 2 + xc) * 2 + core
        x_in[h, d] = push((h, index), ax_ss, ax_rs, 4 * h + d, x_peer)
        c_in[h].append(push((h, index), ac_ss, ac_rs, 8 * h + d, sibling))

    def gather_rows(h):
        for copy in c_in[h]:
            copy.wait_recv()
        for k in range(8):
            block = ag[h, :, k * 16 : (k + 1) * 16, :].astype(f32)
            to = h * 2048 + k * 256
            lhs[:, to : to + 128] = block[:, :8].reshape(128, HD).astype(bf16)
            lhs[:, to + 128 : to + 256] = block[:, 8:].reshape(128, HD).astype(bf16)

    for d in (1, 3, 2):
        pass_z(0, d)
    for d in (0, 1, 3, 2):
        pass_x(0, d)
    for d in (1, 3, 2):
        pass_z(1, d)
    local_copies[1 + HELD].wait()
    gather_rows(0)
    for d in (0, 1, 3, 2):
        pass_x(1, d)
    for n in range(2):
        terms[n] = jnp.dot(
            lhs[:, :2048], w[:2048, n * 256 : (n + 1) * 256], preferred_element_type=f32
        )
    gather_rows(1)

    theirs = pl.multiple_of((1 - y) * 64, 64)
    mine = pl.multiple_of(y * 64, 64)
    y_copies = []
    for n in range(2):
        terms[n] += jnp.dot(
            lhs[:, 2048:], w[2048:, n * 256 : (n + 1) * 256], preferred_element_type=f32
        )
        y_send[n] = terms[n, pl.ds(theirs, 64), :].astype(bf16)
        copy = pltpu.make_async_remote_copy(
            src_ref=y_send.at[n],
            dst_ref=y_recv.at[n],
            send_sem=y_ss.at[n],
            recv_sem=y_rs.at[n],
            device_id=(wide, 1 - y),
            device_id_type=MESH,
        )
        copy.start()
        y_copies.append(copy)
    finals = []
    for n in range(2):
        y_copies[n].wait_recv()
        total = terms[n, pl.ds(mine, 64), :] + y_recv[n].astype(f32)
        finals += [total[:, :HD].astype(bf16), total[:, HD:].astype(bf16)]
    o_ref[...] = jnp.dot(
        out_p[...], jnp.concatenate(finals, axis=0), preferred_element_type=f32
    ).astype(bf16)

    for copy in [*sends, *y_copies, *q_copies.values(), *forwards.values(), *swaps, *results[0], *results[1]]:
        copy.wait_send()


def fused_device(
    queries,
    new_kv,
    suffix_cache,
    suffix_len,
    prefix_cache,
    prompt_len,
    prompt_slot,
    sample_prompt,
    out_weight,
):
    f32, bf16 = jnp.float32, jnp.bfloat16
    q_rows = queries.reshape(HELD, STEPS, KVL * GROUP, HD).transpose(0, 2, 1, 3)
    q_rows = q_rows.reshape(HELD, SPAN, HD)
    new_rows = new_kv.reshape(HELD, STEPS, KVL, 2, HD).transpose(0, 1, 3, 2, 4)
    new_rows = new_rows.reshape(HELD, STEPS * 8, HD)
    suf = suffix_cache.reshape(HELD, SUF, KVL, 2, HD).transpose(0, 1, 3, 2, 4)
    suf = suf.reshape(HELD, SUF * 8, HD)
    pre = prefix_cache.reshape(PSH, KVL, 2, HD).transpose(0, 2, 1, 3).reshape(PSH * 8, HD)
    vm, sm, hbm = pltpu.VMEM, pltpu.SMEM, pl.ANY
    dma = pltpu.SemaphoreType.DMA
    half = (CHIPS, MOST, 2, ROWS, HD)
    block, stat = vm((2, CHIPS, PAIR, HD), bf16), vm((2, CHIPS, 1, HD), f32)
    scratch = [
        vm((HELD, LOCAL, HD), bf16),
        vm((PSH * 8, HD), bf16),
        vm((KVL * 1024, 512), bf16),
        vm((256, 256), bf16),
        vm((128, 128), bf16),
        vm((256, 256), bf16),
        vm((2 * SPAN, WING), jnp.int32),
        vm((8, PSH, HD), bf16),
        block,
        vm((2, 2, CHIPS, PAIR, HD), bf16),
        vm((HELD, SPAN, HD), f32),
        vm((HELD, SPAN, HD), f32),
        vm((HELD, SPAN, HD), f32),
        vm(half, f32),
        vm(half, f32),
        vm(half, f32),
        block,
        stat,
        block,
        stat,
        block,
        stat,
        vm((CHIPS, PAIR, HD), bf16),
        vm((CHIPS, 1, HD), f32),
        vm((CHIPS, PAIR, HD), bf16),
        vm((CHIPS, 1, HD), f32),
        vm((2, 16, 128, HD), bf16),
        vm((128, 4096), bf16),
        vm((2, 128, 256), f32),
        vm((2, 64, 256), bf16),
        vm((2, 64, 256), bf16),
        dma((2 + HELD,)),
    ]
    for count in (16, 16, 4, 16, 16, 8, 8, 16, 2):
        scratch += [dma((count,)), dma((count,))]
    out = pl.pallas_call(
        fused_kernel,
        out_shape=jax.ShapeDtypeStruct((256, HD), bf16),
        in_specs=[pl.BlockSpec(memory_space=sm)] * 4
        + [pl.BlockSpec(memory_space=vm)] * 2
        + [pl.BlockSpec(memory_space=hbm)] * 3,
        out_specs=pl.BlockSpec(memory_space=vm),
        scratch_shapes=scratch,
        compiler_params=pltpu.CompilerParams(
            collective_id=0, has_side_effects=True, vmem_limit_bytes=56 * 1024 * 1024
        ),
        cost_estimate=pl.CostEstimate(
            flops=4_000_000_000, bytes_accessed=12_000_000, transcendentals=1_500_000
        ),
    )(
        suffix_len,
        prompt_len,
        prompt_slot,
        sample_prompt.reshape(-1),
        q_rows,
        new_rows,
        suf,
        pre,
        out_weight,
    )
    return out.reshape(32, 4, STEPS, HD).transpose(0, 2, 1, 3).reshape(32, STEPS, 512)


def solution(mesh):
    small = mesh.shape["wide"] == 2 * CHIPS and mesh.shape["kv"] == 2
    return jax.shard_map(
        fused_device if small else general_device,
        mesh=mesh,
        in_specs=(
            P("wide", None, "kv"),
            P("wide", None, "kv", None),
            P("wide", None, "kv", None),
            P("wide"),
            P("wide", "kv", None),
            P(),
            P(),
            P(),
            P("kv", "wide"),
        ),
        out_specs=P("kv", None, "wide"),
        check_vma=False,
    )
```

```python
import functools
import math

import jax
import jax.numpy as jnp
from jax import lax
from jax.experimental import pallas as pl
from jax.experimental.pallas import tpu as pltpu
from jax.sharding import PartitionSpec as P

HD = 128
GROUP = 8
STEPS = 2
PSH = 512
SUF = 512
NPROMPT = 8
MOST = 2


def sample_ranks(prompt_block):
    length = prompt_block.shape[-1]
    earlier = jnp.arange(length)[None, :] < jnp.arange(length)[:, None]
    matching = prompt_block[..., :, None] == prompt_block[..., None, :]
    return jnp.sum(matching & earlier, axis=-1)


def prefix_part(slots, prefix_cache, prompt_rows, segment):
    sources = slots.shape[0]
    item_count = slots.shape[1]
    kv_local = prefix_cache.shape[1]
    batch_rows = sources * item_count * STEPS
    scale = HD ** (-0.5)
    key_rows = prefix_cache[:, :, :HD]
    value_rows = prefix_cache[:, :, HD:]
    usable = segment * PSH + jnp.arange(PSH) < prompt_rows
    block_rows = math.gcd(batch_rows, max(1, 512 // (kv_local * GROUP)))

    def one_block(query_block):
        scores = (
            jnp.einsum("bgxd,jgd->bgxj", query_block, key_rows, preferred_element_type=jnp.float32)
            * scale
        )
        masked = jnp.where(usable, scores, -1e30)
        row_max = jnp.max(masked, axis=-1)
        weights = jnp.where(usable, jnp.exp(masked - row_max[..., None]), 0.0)
        row_sum = jnp.sum(weights, axis=-1)
        weights_bf = (weights / jnp.maximum(row_sum, 1.0)[..., None]).astype(jnp.bfloat16)
        result = jnp.einsum(
            "bgxj,jgd->bgxd", weights_bf, value_rows, preferred_element_type=jnp.float32
        )
        return (result.astype(jnp.bfloat16), row_max, row_sum)

    query_blocks = slots.reshape(batch_rows // block_rows, block_rows, kv_local, GROUP, HD)
    results = lax.map(one_block, query_blocks)
    part_out = results[0].reshape(sources, item_count, -1)
    part_max = results[1].reshape(sources, item_count, -1)
    part_sum = results[2].reshape(sources, item_count, -1)
    part_out = lax.all_to_all(part_out, "wide", split_axis=0, concat_axis=0, tiled=True)
    part_max, part_sum = (
        lax.all_to_all(part_max, "wide", split_axis=0, concat_axis=0, tiled=True),
        lax.all_to_all(part_sum, "wide", split_axis=0, concat_axis=0, tiled=True),
    )
    return (part_out, part_max, part_sum)


def general_device(
    queries,
    new_kv,
    suffix_cache,
    suffix_len,
    prefix_cache,
    prompt_len,
    prompt_slot,
    sample_prompt,
    out_weight,
):
    wide_count = lax.axis_size("wide")
    split_count = wide_count // NPROMPT
    position = lax.axis_index("wide")
    held_rows = queries.shape[0]
    kv_local = new_kv.shape[2]
    scale = HD ** (-0.5)
    prompt_ids = sample_prompt[:, 0]
    my_prompts = lax.dynamic_slice_in_dim(prompt_ids, position * held_rows, held_rows)
    prompt_range = jnp.arange(NPROMPT)
    slot_range = jnp.arange(MOST)
    my_group = jnp.sum(
        jnp.where(my_prompts[:, None] == prompt_range[None, :], prompt_slot[None, :], 0), axis=1
    )
    my_rank = sample_ranks(my_prompts)
    picked = (my_group[:, None, None] == prompt_range[None, :, None]) & (
        my_rank[:, None, None] == slot_range[None, None, :]
    )
    own_group = position // split_count
    segment = position % split_count
    owner_match = prompt_slot == own_group
    prompt_rows = jnp.sum(jnp.where(owner_match, prompt_len, 0))
    own_prompt = jnp.sum(jnp.where(owner_match, prompt_range, 0))
    flat_queries = queries.reshape(held_rows, -1)
    everyone = lax.all_gather(flat_queries, "wide", axis=0, tiled=True)
    blocks = prompt_ids.reshape(wide_count, held_rows)
    block_rank = sample_ranks(blocks)
    chosen = (blocks[:, :, None] == own_prompt) & (
        block_rank[:, :, None] == slot_range[None, None, :]
    )
    incoming = jnp.einsum(
        "hrc,hrx->hcx",
        chosen.astype(jnp.bfloat16),
        everyone.reshape(wide_count, held_rows, -1),
        preferred_element_type=jnp.float32,
    ).astype(jnp.bfloat16)
    part_out, part_max, part_sum = prefix_part(incoming, prefix_cache, prompt_rows, segment)
    picked_bf = picked.astype(jnp.bfloat16)
    picked_f32 = picked.astype(jnp.float32)
    prefix_out = jnp.einsum(
        "rgc,gscx->rsx",
        picked_bf,
        part_out.reshape(NPROMPT, split_count, MOST, -1),
        preferred_element_type=jnp.float32,
    )
    prefix_max = jnp.einsum(
        "rgc,gscy->rsy",
        picked_f32,
        part_max.reshape(NPROMPT, split_count, MOST, -1),
        precision=lax.Precision.HIGHEST,
    )
    prefix_sum = jnp.einsum(
        "rgc,gscy->rsy",
        picked_f32,
        part_sum.reshape(NPROMPT, split_count, MOST, -1),
        precision=lax.Precision.HIGHEST,
    )
    prefix_out = prefix_out.reshape(held_rows, split_count, STEPS, kv_local, GROUP, HD)
    prefix_max = prefix_max.reshape(held_rows, split_count, STEPS, kv_local, GROUP)
    prefix_sum = prefix_sum.reshape(held_rows, split_count, STEPS, kv_local, GROUP)
    query_rows = queries.reshape(held_rows, STEPS, kv_local, GROUP, HD)
    local_rows = jnp.concatenate([suffix_cache, new_kv], axis=1)
    local_scores = (
        jnp.einsum(
            "stgxd,sjgd->stgxj",
            query_rows,
            local_rows[..., :HD],
            preferred_element_type=jnp.float32,
        )
        * scale
    )
    positions = jnp.arange(SUF + STEPS)
    step_ids = jnp.arange(STEPS)
    local_ok = jnp.where(
        positions[None, None, :] < SUF,
        positions[None, None, :] < suffix_len[:, None, None],
        positions[None, None, :] - SUF <= step_ids[None, :, None],
    )
    local_ok = local_ok[:, :, None, None, :]
    local_masked = jnp.where(local_ok, local_scores, -1e30)
    local_max = jnp.max(local_masked, axis=-1)
    local_weights = jnp.where(local_ok, jnp.exp(local_masked - local_max[..., None]), 0.0)
    local_sum = jnp.sum(local_weights, axis=-1)
    local_bf = (local_weights / local_sum[..., None]).astype(jnp.bfloat16)
    local_out = jnp.einsum(
        "stgxj,sjgd->stgxd", local_bf, local_rows[..., HD:], preferred_element_type=jnp.float32
    )
    overall = jnp.maximum(jnp.max(prefix_max, axis=1), local_max)
    seg_weight = prefix_sum * jnp.exp(prefix_max - overall[:, None])
    local_weight = local_sum * jnp.exp(local_max - overall)
    numerator = (
        jnp.sum(seg_weight[..., None] * prefix_out, axis=1) + local_weight[..., None] * local_out
    )
    denominator = jnp.sum(seg_weight, axis=1) + local_weight
    attn = (numerator / denominator[..., None]).astype(jnp.bfloat16).reshape(held_rows, STEPS, -1)
    terms = jnp.einsum(
        "stk,kd->std",
        lax.all_gather(attn, "wide", axis=0, tiled=True),
        out_weight,
        preferred_element_type=jnp.float32,
    )
    summed = lax.psum_scatter(terms, "kv", scatter_dimension=0, tiled=True)
    return summed.astype(jnp.bfloat16)


MESH = pl.DeviceIdType.MESH
CHIPS = 8
HELD = 4
KVL = 4
ROWS = STEPS * GROUP
SPAN = KVL * ROWS
PART = SPAN // 2
PAIR = MOST * PART
SUF_ROWS = SUF * 2 * KVL
LOCAL = SUF_ROWS + 128
FAR = 1 << 20
SCALE2 = HD ** (-0.5) * math.log2(math.e)
NT = (((1,), (1,)), ((), ()))


def fused_kernel(
    slen_ref,
    plen_ref,
    pslot_ref,
    sprompt_ref,
    q_ref,
    new_ref,
    suf_hbm,
    pre_hbm,
    w_hbm,
    o_ref,
    suf,
    pre,
    w,
    split_p,
    turn_p,
    out_p,
    place,
    pkv,
    qslot,
    qrecv,
    lo,
    lm,
    ll,
    half_o,
    half_m,
    half_l,
    so_send,
    st_send,
    so_recv,
    st_recv,
    co_send,
    cs_send,
    co_first,
    cs_first,
    co_second,
    cs_second,
    ag,
    lhs,
    terms,
    y_send,
    y_recv,
    loc_sem,
    q_ss,
    q_rs,
    qf_ss,
    qf_rs,
    x_ss,
    x_rs,
    c_ss,
    c_rs,
    s_ss,
    s_rs,
    z_ss,
    z_rs,
    ax_ss,
    ax_rs,
    ac_ss,
    ac_rs,
    y_ss,
    y_rs,
):
    f32, bf16 = jnp.float32, jnp.bfloat16
    wide = lax.axis_index("wide")
    y = lax.axis_index("kv")
    chip = wide // 2
    core = wide % 2
    zc = chip // 2
    xc = chip % 2
    sibling = (chip * 2 + 1 - core, y)

    def at_chip(c):
        return (c * 2 + core, y)

    local_copies = [pltpu.make_async_copy(pre_hbm, pre, loc_sem.at[0])]
    local_copies += [
        pltpu.make_async_copy(
            suf_hbm.at[s], suf.at[s, pl.ds(0, SUF_ROWS)], loc_sem.at[1 + s]
        ) for s in range(HELD)
    ]
    local_copies.append(pltpu.make_async_copy(w_hbm, w, loc_sem.at[1 + HELD]))
    for copy in local_copies:
        copy.start()

    barrier = pltpu.get_barrier_semaphore()
    for d in range(1, CHIPS):
        pl.semaphore_signal(
            barrier, inc=1, device_id=at_chip((chip + d) % CHIPS), device_id_type=MESH
        )
    pl.semaphore_signal(barrier, inc=1, device_id=sibling, device_id_type=MESH)
    pl.semaphore_signal(barrier, inc=1, device_id=(wide, 1 - y), device_id_type=MESH)

    prompts = [sprompt_ref[wide * HELD + s] for s in range(HELD)]
    groups = [pslot_ref[p] for p in prompts]
    ranks = []
    for s in range(HELD):
        rank = jnp.int32(0)
        for e in range(s):
            rank = rank + jnp.where(prompts[e] == prompts[s], 1, 0)
        ranks.append(rank)
    for c in range(CHIPS):
        for m in range(MOST):
            pick = jnp.int32(0)
            for s in range(1, HELD):
                pick = pick + jnp.where((groups[s] == c) & (ranks[s] == m), s, 0)
            chosen = q_ref[pick]
            for h in range(2):
                qslot[h, c, m * PART : (m + 1) * PART, :] = chosen[h * PART : (h + 1) * PART]
    prompt_rows = jnp.int32(0)
    for p in range(NPROMPT):
        prompt_rows = prompt_rows + jnp.where(pslot_ref[p] == chip, plen_ref[p], 0)

    pl.semaphore_wait(barrier, CHIPS + 1)

    q_copies = {}
    for h in range(2):
        for d in (4, 3, 5, 2, 6, 1, 7):
            dst = (chip + d) % CHIPS
            q_copies[h, d] = pltpu.make_async_remote_copy(
                src_ref=qslot.at[h, dst],
                dst_ref=qrecv.at[h, core, chip],
                send_sem=q_ss.at[8 * h + d],
                recv_sem=q_rs.at[8 * h + d],
                device_id=at_chip(dst),
                device_id_type=MESH,
            )
            q_copies[h, d].start()
        qrecv[h, core, chip] = qslot[h, chip]
    forwards = {}

    def forward(h, d):
        src = (chip + CHIPS - d) % CHIPS
        if d:
            q_copies[h, d].wait_recv()
        forwards[h, d] = pltpu.make_async_remote_copy(
            src_ref=qrecv.at[h, core, src],
            dst_ref=qrecv.at[h, core, src],
            send_sem=qf_ss.at[8 * h + d],
            recv_sem=qf_rs.at[8 * h + d],
            device_id=sibling,
            device_id_type=MESH,
        )
        forwards[h, d].start()

    forward(0, 0)
    forward(1, 0)

    out_row = lax.broadcasted_iota(jnp.int32, (256, 256), 0)
    in_row = lax.broadcasted_iota(jnp.int32, (256, 256), 1)
    split_p[...] = jnp.where(in_row == (out_row & 31) * 8 + (out_row >> 5), 1.0, 0.0).astype(bf16)
    gathered = ((out_row >> 1) & 3) * 64 + (out_row >> 3) * 2 + (out_row & 1)
    out_p[...] = jnp.where(in_row == gathered, 1.0, 0.0).astype(bf16)
    to_row, from_row = out_row[:128, :128], in_row[:128, :128]
    source = ((to_row >> 1) & 3) * PART + (to_row >> 3) * 2 + (to_row & 1)
    turn_p[...] = jnp.where(from_row == source, 1.0, 0.0).astype(bf16)

    local_copies[0].wait()
    for i in range(8):
        rows = jnp.concatenate(
            [pre[i * 512 : i * 512 + 256, :], pre[i * 512 + 256 : (i + 1) * 512, :]], axis=1
        )
        parted = jnp.dot(split_p[...], rows, preferred_element_type=f32).astype(bf16)
        for k in range(8):
            pkv[k, i * 64 : i * 64 + 32, :] = parted[k * 32 : (k + 1) * 32, :HD]
            pkv[k, i * 64 + 32 : (i + 1) * 64, :] = parted[k * 32 : (k + 1) * 32, HD:]

    col = lax.broadcasted_iota(jnp.int32, (SPAN, LOCAL), 1)
    row = lax.broadcasted_iota(jnp.int32, (SPAN, LOCAL), 0)
    spot = col >> 3
    fresh = jnp.where(spot - SUF <= (row & 1), -1, FAR)
    place[...] = jnp.where((col & 7) == (row >> 4), jnp.where(spot < SUF, spot, fresh), FAR)

    def local_part(*samples):
        for s in samples:
            local_copies[1 + s].wait()
            suf[s, SUF_ROWS : SUF_ROWS + 16, :] = new_ref[s]
            suf[s, SUF_ROWS + 16 :, :] = jnp.zeros((LOCAL - SUF_ROWS - 16, HD), bf16)
        scores = [
            lax.dot_general(q_ref[s], suf[s], NT, preferred_element_type=f32) for s in samples
        ]
        for s, score in zip(samples, scores):
            masked = jnp.where(place[...] < slen_ref[s], score * SCALE2, -1e30)
            top = jnp.max(masked, axis=1, keepdims=True)
            weights = jnp.exp2(masked - top)
            total = jnp.sum(weights, axis=1, keepdims=True)
            moved = pltpu.roll(weights, KVL, 1).astype(bf16)
            lo[s] = jnp.dot(moved, suf[s], preferred_element_type=f32)
            lm[s] = jnp.broadcast_to(top, (SPAN, HD))
            ll[s] = jnp.broadcast_to(total, (SPAN, HD))

    local_part(0)
    for d in (1, 7, 2, 6, 3, 5, 4):
        forward(0, d)
    local_part(1)

    usable = lax.broadcasted_iota(jnp.int32, (256, PSH), 1) < prompt_rows - core * PSH

    def prefix_half(h, which):
        queries = qrecv[h, which].reshape(CHIPS, MOST, 2, ROWS, HD)
        for e in range(2):
            g = 2 * h + e
            query = queries[:, :, e].reshape(256, HD)
            scores = lax.dot_general(query, pkv[g], NT, preferred_element_type=f32)
            masked = jnp.where(usable, scores * SCALE2, -1e30)
            top = jnp.max(masked, axis=1, keepdims=True)
            weights = jnp.exp2(masked - top)
            total = jnp.sum(weights, axis=1, keepdims=True)
            result = jnp.dot(weights.astype(bf16), pkv[KVL + g], preferred_element_type=f32)
            shape = (CHIPS, MOST, ROWS, HD)
            half_o[:, :, e] = result.reshape(shape)
            half_m[:, :, e] = jnp.broadcast_to(top, (256, HD)).reshape(shape)
            half_l[:, :, e] = jnp.broadcast_to(total, (256, HD)).reshape(shape)

    def stat_rows(top, total):
        return jnp.concatenate([top, total], axis=0).T[:1]

    def flat(ref, c):
        return ref[c].reshape(PAIR, HD)

    co_recv, cs_recv = (co_first, co_second), (cs_first, cs_second)
    swaps = []
    results = {}

    def merge(h, c):
        m1, l1 = flat(half_m, c), flat(half_l, c)
        other = jnp.broadcast_to(st_recv[h, c][0:1], (HD, HD)).T
        m2, l2 = other[:PAIR], other[PAIR:]
        top = jnp.maximum(m1, m2)
        w1, w2 = jnp.exp2(m1 - top), jnp.exp2(m2 - top)
        total = w1 * l1 + w2 * l2
        mixed = w1 * flat(half_o, c) + w2 * so_recv[h, c].astype(f32)
        return (mixed / total).astype(bf16), stat_rows(top, total)

    def prefix_part(h):
        for d in range(CHIPS):
            forwards[h, d].wait_recv()
        prefix_half(h, 1 - core)
        for c in range(CHIPS):
            so_send[h, c] = flat(half_o, c).astype(bf16)
            st_send[h, c] = stat_rows(flat(half_m, c), flat(half_l, c))
        mine = []
        for i, (src, dst) in enumerate(((so_send, so_recv), (st_send, st_recv))):
            copy = pltpu.make_async_remote_copy(
                src_ref=src.at[h],
                dst_ref=dst.at[h],
                send_sem=x_ss.at[2 * h + i],
                recv_sem=x_rs.at[2 * h + i],
                device_id=sibling,
                device_id_type=MESH,
            )
            copy.start()
            mine.append(copy)
        swaps.extend(mine)
        prefix_half(h, core)
        if h == 0:
            for d in (1, 7, 2, 6, 3, 5, 4):
                forward(1, d)
        for copy in mine:
            copy.wait_recv()
        for d in (4, 3, 5, 2, 6, 1, 7):
            dst = (chip + d) % CHIPS
            co_send[h, dst], cs_send[h, dst] = merge(h, dst)
            for src, target, ss, rs in (
                (co_send, co_recv, c_ss, c_rs),
                (cs_send, cs_recv, s_ss, s_rs),
            ):
                copy = pltpu.make_async_remote_copy(
                    src_ref=src.at[h, dst],
                    dst_ref=target[h].at[chip],
                    send_sem=ss.at[8 * h + d],
                    recv_sem=rs.at[8 * h + d],
                    device_id=at_chip(dst),
                    device_id_type=MESH,
                )
                copy.start()
                results.setdefault(h, []).append(copy)
        co_recv[h][chip], cs_recv[h][chip] = merge(h, chip)

    prefix_part(0)
    prefix_part(1)
    local_part(2, 3)

    def attention(h):
        for copy in results[h]:
            copy.wait_recv()
        here = slice(h * PART, (h + 1) * PART)
        parts = []
        for s in range(HELD):
            stats = jnp.broadcast_to(cs_recv[h][groups[s]][0:1], (HD, HD)).T
            block = co_recv[h][groups[s]].astype(f32)
            first = jnp.broadcast_to(ranks[s] == 0, (PART, HD))
            pm = jnp.where(first, stats[:PART], stats[PART:PAIR])
            pt = jnp.where(first, stats[PAIR : PAIR + PART], stats[PAIR + PART :])
            po = jnp.where(first, block[:PART], block[PART:])
            own = lm[s, here, :]
            overall = jnp.maximum(pm, own)
            wp = pt * jnp.exp2(pm - overall)
            wl = jnp.exp2(own - overall)
            mixed = wp * po + wl * lo[s, here, :]
            parts.append((mixed / (wp + wl * ll[s, here, :])).astype(bf16))
        attn = jnp.concatenate(parts, axis=0)
        turned = jnp.dot(turn_p[...], attn, preferred_element_type=f32)
        ag[h, wide] = turned.astype(bf16)

    sends = []

    def push(index, ss, rs, i, device):
        copy = pltpu.make_async_remote_copy(
            src_ref=ag.at[index],
            dst_ref=ag.at[index],
            send_sem=ss.at[i],
            recv_sem=rs.at[i],
            device_id=device,
            device_id_type=MESH,
        )
        copy.start()
        sends.append(copy)
        return copy

    x_peer = at_chip(zc * 2 + 1 - xc)
    z_in, x_in, c_in = {}, {}, ([], [])
    for h in range(2):
        attention(h)
        x_in[h, 0] = push((h, wide), ax_ss, ax_rs, 4 * h, x_peer)
        for d in (2, 1, 3):
            device = at_chip(((zc + d) % 4) * 2 + xc)
            z_in[h, d] = push((h, wide), z_ss, z_rs, 4 * h + d, device)
        c_in[h].append(push((h, wide), ac_ss, ac_rs, 8 * h, sibling))

    def pass_x(h, d):
        x_in[h, d].wait_recv()
        index = (((zc + 4 - d) % 4) * 2 + 1 - xc) * 2 + core
        c_in[h].append(push((h, index), ac_ss, ac_rs, 8 * h + 4 + d, sibling))

    def pass_z(h, d):
        z_in[h, d].wait_recv()
        index = (((zc + 4 - d) % 4) * 2 + xc) * 2 + core
        x_in[h, d] = push((h, index), ax_ss, ax_rs, 4 * h + d, x_peer)
        c_in[h].append(push((h, index), ac_ss, ac_rs, 8 * h + d, sibling))

    def gather_rows(h):
        for copy in c_in[h]:
            copy.wait_recv()
        for k in range(8):
            block = ag[h, :, k * 16 : (k + 1) * 16, :].astype(f32)
            to = h * 2048 + k * 256
            lhs[:, to : to + 128] = block[:, :8].reshape(128, HD).astype(bf16)
            lhs[:, to + 128 : to + 256] = block[:, 8:].reshape(128, HD).astype(bf16)

    for d in (1, 3, 2):
        pass_z(0, d)
    for d in (0, 1, 3, 2):
        pass_x(0, d)
    for d in (1, 3, 2):
        pass_z(1, d)
    local_copies[1 + HELD].wait()
    gather_rows(0)
    for d in (0, 1, 3, 2):
        pass_x(1, d)
    for n in range(2):
        terms[n] = jnp.dot(
            lhs[:, :2048], w[:2048, n * 256 : (n + 1) * 256], preferred_element_type=f32
        )
    gather_rows(1)

    theirs = pl.multiple_of((1 - y) * 64, 64)
    mine = pl.multiple_of(y * 64, 64)
    y_copies = []
    for n in range(2):
        terms[n] += jnp.dot(
            lhs[:, 2048:], w[2048:, n * 256 : (n + 1) * 256], preferred_element_type=f32
        )
        y_send[n] = terms[n, pl.ds(theirs, 64), :].astype(bf16)
        copy = pltpu.make_async_remote_copy(
            src_ref=y_send.at[n],
            dst_ref=y_recv.at[n],
            send_sem=y_ss.at[n],
            recv_sem=y_rs.at[n],
            device_id=(wide, 1 - y),
            device_id_type=MESH,
        )
        copy.start()
        y_copies.append(copy)
    finals = []
    for n in range(2):
        y_copies[n].wait_recv()
        total = terms[n, pl.ds(mine, 64), :] + y_recv[n].astype(f32)
        finals += [total[:, :HD].astype(bf16), total[:, HD:].astype(bf16)]
    o_ref[...] = jnp.dot(
        out_p[...], jnp.concatenate(finals, axis=0), preferred_element_type=f32
    ).astype(bf16)

    for copy in [*sends, *y_copies, *q_copies.values(), *forwards.values(), *swaps, *results[0], *results[1]]:
        copy.wait_send()


def fused_device(
    queries,
    new_kv,
    suffix_cache,
    suffix_len,
    prefix_cache,
    prompt_len,
    prompt_slot,
    sample_prompt,
    out_weight,
):
    f32, bf16 = jnp.float32, jnp.bfloat16
    q_rows = queries.reshape(HELD, STEPS, KVL * GROUP, HD).transpose(0, 2, 1, 3)
    q_rows = q_rows.reshape(HELD, SPAN, HD)
    new_rows = new_kv.reshape(HELD, STEPS, KVL, 2, HD).transpose(0, 1, 3, 2, 4)
    new_rows = new_rows.reshape(HELD, STEPS * 8, HD)
    suf = suffix_cache.reshape(HELD, SUF, KVL, 2, HD).transpose(0, 1, 3, 2, 4)
    suf = suf.reshape(HELD, SUF * 8, HD)
    pre = prefix_cache.reshape(PSH, KVL, 2, HD).transpose(0, 2, 1, 3).reshape(PSH * 8, HD)
    vm, sm, hbm = pltpu.VMEM, pltpu.SMEM, pl.ANY
    dma = pltpu.SemaphoreType.DMA
    half = (CHIPS, MOST, 2, ROWS, HD)
    block, stat = vm((2, CHIPS, PAIR, HD), bf16), vm((2, CHIPS, 1, HD), f32)
    scratch = [
        vm((HELD, LOCAL, HD), bf16),
        vm((PSH * 8, HD), bf16),
        vm((KVL * 1024, 512), bf16),
        vm((256, 256), bf16),
        vm((128, 128), bf16),
        vm((256, 256), bf16),
        vm((SPAN, LOCAL), jnp.int32),
        vm((8, PSH, HD), bf16),
        block,
        vm((2, 2, CHIPS, PAIR, HD), bf16),
        vm((HELD, SPAN, HD), f32),
        vm((HELD, SPAN, HD), f32),
        vm((HELD, SPAN, HD), f32),
        vm(half, f32),
        vm(half, f32),
        vm(half, f32),
        block,
        stat,
        block,
        stat,
        block,
        stat,
        vm((CHIPS, PAIR, HD), bf16),
        vm((CHIPS, 1, HD), f32),
        vm((CHIPS, PAIR, HD), bf16),
        vm((CHIPS, 1, HD), f32),
        vm((2, 16, 128, HD), bf16),
        vm((128, 4096), bf16),
        vm((2, 128, 256), f32),
        vm((2, 64, 256), bf16),
        vm((2, 64, 256), bf16),
        dma((2 + HELD,)),
    ]
    for count in (16, 16, 4, 16, 16, 8, 8, 16, 2):
        scratch += [dma((count,)), dma((count,))]
    out = pl.pallas_call(
        fused_kernel,
        out_shape=jax.ShapeDtypeStruct((256, HD), bf16),
        in_specs=[pl.BlockSpec(memory_space=sm)] * 4
        + [pl.BlockSpec(memory_space=vm)] * 2
        + [pl.BlockSpec(memory_space=hbm)] * 3,
        out_specs=pl.BlockSpec(memory_space=vm),
        scratch_shapes=scratch,
        compiler_params=pltpu.CompilerParams(
            collective_id=0, has_side_effects=True, vmem_limit_bytes=56 * 1024 * 1024
        ),
        cost_estimate=pl.CostEstimate(
            flops=4_000_000_000, bytes_accessed=12_000_000, transcendentals=1_500_000
        ),
    )(
        suffix_len,
        prompt_len,
        prompt_slot,
        sample_prompt.reshape(-1),
        q_rows,
        new_rows,
        suf,
        pre,
        out_weight,
    )
    return out.reshape(32, 4, STEPS, HD).transpose(0, 2, 1, 3).reshape(32, STEPS, 512)


def solution(mesh):
    small = mesh.shape["wide"] == 2 * CHIPS and mesh.shape["kv"] == 2
    return jax.shard_map(
        fused_device if small else general_device,
        mesh=mesh,
        in_specs=(
            P("wide", None, "kv"),
            P("wide", None, "kv", None),
            P("wide", None, "kv", None),
            P("wide"),
            P("wide", "kv", None),
            P(),
            P(),
            P(),
            P("kv", "wide"),
        ),
        out_specs=P("kv", None, "wide"),
        check_vma=False,
    )
```
